128 devices in a mesh: sub: 8 (over y, core), beam: 16 (over x, z).
Axes of the slice: x: 4, y: 4, z: 4, core: 2. Of those that a mesh axis runs over, the one named last changes fastest.
Arguments:
- subimage: float32 [8, 256, 2, 16384], P('sub', 'beam'), may hold values from -6 to 6
- pulses: float32 [2, 8, 16, 16, 2, 16384], P(None, 'sub', 'beam'), may hold values from -6 to 6
- ingest_owner: int32 [2, 8], P(None, 'sub'), may hold values from 0 to 15
- weights: float32 [2, 8, 256, 2, 16], P(None, 'sub', 'beam'), may hold values from -1 to 1
- offsets: int32 [2, 8, 256], P(None, 'sub', 'beam'), may hold values from 0 to 256
- filter_taps: float32 [2, 8, 256, 8], P(None, 'sub', 'beam'), may hold values from -2 to 2
- cycles: int32 [2, 8, 256], P(None, 'sub', 'beam'), may hold values from 0 to 16383
- merge_phase: float32 [2, 8, 256], P(None, 'sub', 'beam'), may hold values from -3.140625 to 3.140625
- destination: int32 [256, 1], P('beam'), may hold values from 0 to 15; in each aligned block of 16 rows (0 to 15, 16 to 31, ...) at most 2 rows name the same one
Outputs:
- regrouped: float32 [8, 512, 2, 16384], P('sub', 'beam')
The draws below stay inside these ranges and needn't reach their ends.
Inputs may be any that keep to these rules, and one draw needn't show every extreme that they name: `destination`: the same owners for every subaperture group; among the rows of one device at most 2 go to one owner, and exactly 2 to some owner.
All inputs are finite; a program needn't handle non-finite values.
Results may differ from the reference program's by a relative error of at most 0.0003.
Values sent between devices are 32-bit elements; how exact they have to be, the bound alone decides.
A program may use at most 128 MiB of HBM per device.

```python
import math
import jax
import jax.numpy as jnp
import numpy as np
from jax import lax

R = 16384
PB = 16
CAP = 2
TAPS = 8
SECTIONS = 2
ROW_DEV = 16
ROWS = 256
NSUBS = 8
SLOTS = 32
MAXOFF = 256
N_BEAM = 16


def touch_ends(entries, rng, least, top_value):
    place = [jax.random.randint(jax.random.fold_in(rng, axis), (), 0, length) for axis, length in enumerate(entries.shape)]
    longest = entries.shape.index(max(entries.shape))
    beside = place[:longest] + [(place[longest] + 1) % entries.shape[longest]] + place[longest + 1:]
    return entries.at[tuple(place)].set(least).at[tuple(beside)].set(top_value)


def shard_levels(rng, extent, split, low, largest):
    loudness, own = 1.0, jax.random.fold_in(rng, 6)
    for position, blocks in split:
        steps = jnp.exp(jax.random.uniform(jax.random.fold_in(own, position), (blocks,), jnp.float32, low / len(split), largest / len(split)))
        loudness = loudness * jnp.repeat(steps, extent[position] // blocks).reshape([-1 if axis == position else 1 for axis in range(len(extent))])
    return loudness


def routed_block(key, own, number, rows, count, top, limit, skew):
    order = jax.random.permutation(key, count)
    heavy_load, common = load_shares(count, rows * top, limit, skew, True), load_shares(count, rows * top, limit, skew, False)
    places = jnp.arange(count)

    def named(lengths, rotation):
        used = int((lengths > 0).sum())
        fixed = max(1, used // 4)
        moved = fixed + (places - fixed + rotation * (used - fixed)) % max(1, count - fixed)
        return jnp.zeros((count,), jnp.int32).at[order[jnp.where(places < fixed, places, moved)]].set(jnp.asarray(lengths, jnp.int32))

    lengths = jnp.where(number % 4 == 0, named(heavy_load, number // 4), named(common, number - number // 4 - 1))
    mixed = jax.random.permutation(jax.random.fold_in(own, 3), count)
    source_of, receiver = mixed[0:count // 2 * 2:2], mixed[1:count // 2 * 2:2]
    room = jnp.minimum(lengths[source_of] - 1, limit - lengths[receiver]) // 2
    room = jnp.where((source_of == order[0]) | (receiver == order[0]) | (lengths[receiver] == 0), 0, jnp.maximum(room, 0))
    moved = jax.random.randint(jax.random.fold_in(own, 4), (count // 2,), 0, 1 << 20) % (room + 1)
    lengths = lengths.at[source_of].add(-moved).at[receiver].add(moved)
    items = jnp.searchsorted(jnp.cumsum(lengths), jnp.arange(rows * top), side="right").astype(jnp.int32)
    listing = items.reshape(top, rows).T
    listing = listing[jax.random.permutation(jax.random.fold_in(own, 1), rows)]
    rotation = jax.random.randint(jax.random.fold_in(own, 2), (rows, 1), 0, top)
    return jnp.take_along_axis(listing, (jnp.arange(top)[None, :] + rotation) % top, axis=1)


def load_shares(count, total, limit, skew, full):
    loads = [(1 << 20) // math.isqrt(standing ** skew) + 1 for standing in range(1, count + 1)]
    largest = limit if full else min(limit, max(-(-total // count), total * loads[0] // sum(loads)))
    least = 1 if total - largest >= count - 1 else 0
    holding, surplus = [largest] + [least] * (count - 1), total - largest - least * (count - 1)
    while surplus > 0:
        candidates = [i for i in range(1, count) if holding[i] < largest] or [i for i in range(1, count) if holding[i] < limit]
        mass, left = sum([loads[i] for i in candidates]), surplus
        for i in candidates:
            addition = min(limit - holding[i], max(1, left * loads[i] // mass), surplus)
            holding[i] = holding[i] + addition
            surplus = surplus - addition
    return np.array(holding)


def noise(key, shape, spread, limit, split=(), kind=jnp.bfloat16):
    loudness = shard_levels(key, shape, split, -0.22, 0.18) if split else 1.0
    result = jax.random.normal(key, shape, jnp.float32) * spread * loudness
    return jnp.minimum(jnp.maximum(result, -limit), limit).astype(kind)


def setup_inputs(seed: int = 0) -> dict:
    streams_of = jax.random.split(jax.random.key(seed), 10)
    subimage = noise(streams_of[0], (NSUBS, ROWS, 2, R), 1.0, 6.0, ((0, 8), (1, 16)), jnp.float32)
    pulses = noise(streams_of[1], (SECTIONS, NSUBS, N_BEAM, PB, 2, R), 1.0, 6.0, ((1, 8), (2, 16)), jnp.float32)
    ingest_owner = touch_ends(jax.random.randint(streams_of[2], (SECTIONS, NSUBS), 0, N_BEAM), jax.random.fold_in(streams_of[2], 1), 0, N_BEAM - 1).astype(jnp.int32)
    weights = noise(streams_of[3], (SECTIONS, NSUBS, ROWS, 2, PB), (2 * PB) ** -0.5, 1.0, ((1, 8), (2, 16)), jnp.float32)
    offsets = touch_ends(jax.random.randint(streams_of[4], (SECTIONS, NSUBS, ROWS), 0, MAXOFF + 1), jax.random.fold_in(streams_of[4], 1), 0, MAXOFF).astype(jnp.int32)
    filter_taps = noise(streams_of[5], (SECTIONS, NSUBS, ROWS, TAPS), TAPS ** -0.5, 2.0, ((1, 8), (2, 16)), jnp.float32)
    cycles = touch_ends(jax.random.randint(streams_of[6], (SECTIONS, NSUBS, ROWS), 0, R), jax.random.fold_in(streams_of[6], 1), 0, R - 1).astype(jnp.int32)
    merge_phase = jnp.clip(jax.random.uniform(streams_of[7], (SECTIONS, NSUBS, ROWS), jnp.float32, -3.140625, 3.140625), -3.140625, 3.140625)
    destination_keys = jax.random.split(jax.random.fold_in(streams_of[8], 1), ROWS // ROW_DEV)
    destination_turns = jax.random.permutation(jax.random.fold_in(streams_of[8], 3), ROWS // ROW_DEV)
    destination = jax.vmap(lambda own, number: routed_block(jax.random.fold_in(streams_of[8], 2), own, number, ROW_DEV, N_BEAM, 1, CAP, 2))(destination_keys, destination_turns).reshape((ROWS, 1))
    return dict(subimage=subimage, pulses=pulses, ingest_owner=ingest_owner, weights=weights, offsets=offsets, filter_taps=filter_taps, cycles=cycles, merge_phase=merge_phase, destination=destination)


TWO_PI = 2.0 * math.pi


def project_rows(received_block, coeffs):
    highest = lax.Precision.HIGHEST
    real_part = jnp.dot(coeffs[:, 0], received_block[:, 0], precision=highest) - jnp.dot(coeffs[:, 1], received_block[:, 1], precision=highest)
    imag_part = jnp.dot(coeffs[:, 0], received_block[:, 1], precision=highest) + jnp.dot(coeffs[:, 1], received_block[:, 0], precision=highest)
    return jnp.stack([real_part, imag_part], axis=1)


def interpolate(row_data, shifts, filters):
    length = row_data.shape[2]
    tap_count = filters.shape[1]
    margin = MAXOFF + tap_count - 1
    padded = jnp.pad(row_data, ((0, 0), (0, 0), (0, margin)))
    windows = jax.vmap(lambda one_row, first_bin: lax.dynamic_slice_in_dim(one_row, first_bin, length + tap_count - 1, axis=1))(padded, shifts.astype(jnp.int32))
    summed = filters[:, 0, None, None] * windows[:, :, 0:length]
    for tap_index in range(1, tap_count):
        summed = summed + filters[:, tap_index, None, None] * windows[:, :, tap_index:tap_index + length]
    return summed


def apply_ramp(row_data, counts):
    length = row_data.shape[2]
    positions = jnp.arange(length, dtype=jnp.int32)
    ramp_angle = ((counts.astype(jnp.int32)[:, None] * positions[None, :]) % length).astype(jnp.float32) * (TWO_PI / length)
    cos_part = jnp.cos(ramp_angle)
    sin_part = jnp.sin(ramp_angle)
    real_part = row_data[:, 0] * cos_part - row_data[:, 1] * sin_part
    imag_part = row_data[:, 0] * sin_part + row_data[:, 1] * cos_part
    return jnp.stack([real_part, imag_part], axis=1)


def rotate_add(own_rows, partner, phase_angle):
    cos_part = jnp.cos(phase_angle)[:, None]
    sin_part = jnp.sin(phase_angle)[:, None]
    real_part = partner[:, 0] * cos_part - partner[:, 1] * sin_part
    imag_part = partner[:, 0] * sin_part + partner[:, 1] * cos_part
    return own_rows + jnp.stack([real_part, imag_part], axis=1)


def one_group(received_block, coeffs, shifts, filters, counts):
    return apply_ramp(interpolate(project_rows(received_block, coeffs), shifts, filters), counts)


def reference(subimage, pulses, ingest_owner, weights, offsets, filter_taps, cycles, merge_phase, destination):
    groups = jnp.arange(NSUBS, dtype=jnp.int32)
    current = subimage
    for section_index in range(SECTIONS):
        blocks = pulses[section_index, groups, ingest_owner[section_index].astype(jnp.int32)]
        projected = jax.vmap(one_group)(blocks, weights[section_index], offsets[section_index], filter_taps[section_index], cycles[section_index])
        current = current + projected
        partner = current[jnp.bitwise_xor(groups, 2 ** section_index)]
        current = jax.vmap(rotate_add)(current, partner, merge_phase[section_index])
    targets = destination[:, 0].astype(jnp.int32).reshape(N_BEAM, ROW_DEV)
    same_owner = targets[:, :, None] == targets[:, None, :]
    earlier = jnp.arange(ROW_DEV, dtype=jnp.int32)[None, :] < jnp.arange(ROW_DEV, dtype=jnp.int32)[:, None]
    earlier_count = jnp.sum((same_owner & earlier[None]).astype(jnp.int32), axis=2)
    source_device = jnp.arange(N_BEAM, dtype=jnp.int32)[:, None]
    placement_index = (targets * SLOTS + source_device * CAP + earlier_count).reshape(ROWS).astype(jnp.int32)
    regrouped = jnp.zeros((NSUBS, N_BEAM * SLOTS, 2, R), jnp.float32).at[:, placement_index].set(current)
    return regrouped
```

```python
import functools
import math

import jax
import jax.numpy as jnp
from jax import lax
from jax.experimental import pallas as pl
from jax.experimental.pallas import tpu as pltpu
from jax.sharding import PartitionSpec as P

CAP = 2
TAPS = 8
PB = 16
ROWS = 16
BEAMS = 16
LANES = 128
SUBL = 256
PAD = 32
CHUNKS = 8
CS = SUBL // CHUNKS
TWO_PI = 2.0 * math.pi
MESH = pl.DeviceIdType.MESH


def swapped(x):
    n = x.shape[0] // 8
    y = x.reshape(n, 8, LANES)
    even = lax.broadcasted_iota(jnp.int32, (n, 8, LANES), 1) % 2 == 0
    z = jnp.where(even, pltpu.roll(y, 7, 1), pltpu.roll(y, 1, 1))
    return z.reshape(x.shape)


def pair_sign(rows):
    even = lax.broadcasted_iota(jnp.int32, (rows, LANES), 0) % 2 == 0
    return jnp.where(even, -1.0, 1.0).astype(jnp.float32)


def merge_kernel(
    weights, offsets, taps, block_cos, block_sin, turn_cos, turn_sin, slot_row, slot_used,
    sub_ref, got_ref, cos_ref, sin_ref,
    out_ref,
    proj, first, first_in, late, second, second_in, merged, slots,
    core_send, core_recv, y_send, y_recv, beam_send, beam_recv, own_sem,
):
    sub = lax.axis_index("sub")
    me = lax.axis_index("beam")
    core_peer = (sub ^ 1, me)
    y_peer = (sub ^ 2, me)

    barrier = pltpu.get_barrier_semaphore()
    pl.semaphore_signal(barrier, inc=1, device_id=core_peer, device_id_type=MESH)
    pl.semaphore_signal(barrier, inc=1, device_id=y_peer, device_id_type=MESH)
    for shift in range(1, BEAMS):
        pl.semaphore_signal(barrier, inc=1, device_id=(sub, me ^ shift), device_id_type=MESH)

    zero = jnp.zeros((PAD, LANES), jnp.float32)
    for s in range(2):
        def clear(g, _, s=s):
            proj[s, g, pl.ds(SUBL, PAD), :] = zero
            return 0
        lax.fori_loop(0, ROWS, clear, 0)

    def project(s, lo):
        def half(h, _):
            acc = [None] * 8
            for p in range(PB):
                b = got_ref[s, p, pl.ds(lo, CS), :]
                t = swapped(b) * pair_sign(CS)
                for k in range(8):
                    at = ((s * ROWS) + h * 8 + k) * 32 + p
                    term = weights[at] * b + weights[at + 16] * t
                    acc[k] = term if acc[k] is None else acc[k] + term
            for k in range(8):
                proj[s, h * 8 + k, pl.ds(lo, CS), :] = acc[k]
            return 0
        lax.fori_loop(0, 2, half, 0)

    lane = lax.broadcasted_iota(jnp.int32, (CS, LANES), 1)
    lane_w = lax.broadcasted_iota(jnp.int32, (CS + 8, LANES), 1)

    def added(s, g, lo):
        off = offsets[s * ROWS + g]
        a = off // LANES
        b = off % LANES
        v = proj[s, g, pl.ds(lo + 2 * a, CS + 8), :]
        u = pltpu.roll(v, lax.rem(LANES - b, LANES), 1)
        up = jnp.concatenate([u[2:], u[:2]], axis=0)
        w = jnp.where(lane_w < LANES - b, u, up)
        here, following = w[:CS], w[2 : CS + 2]
        base = (s * ROWS + g) * TAPS
        acc = taps[base] * here
        for k in range(1, TAPS):
            acc = acc + taps[base + k] * pltpu.roll(jnp.where(lane < k, following, here), LANES - k, 1)
        c0 = cos_ref[s, g]
        s0 = sin_ref[s, g]
        sign = pair_sign(8)
        parts = []
        turned = swapped(acc)
        for v8 in range(CS // 8):
            at = (s * ROWS + g) * (SUBL // 8) + lo // 8 + v8
            ci = block_cos[at]
            si = block_sin[at]
            cc = c0 * ci - s0 * si
            ss = (s0 * ci + c0 * si) * sign
            parts.append(acc[v8 * 8 : v8 * 8 + 8] * cc + turned[v8 * 8 : v8 * 8 + 8] * ss)
        return jnp.concatenate(parts, axis=0)

    def copy_core(c):
        return pltpu.make_async_remote_copy(
            src_ref=first.at[:, pl.ds(c * CS, CS), :], dst_ref=first_in.at[:, pl.ds(c * CS, CS), :],
            send_sem=core_send.at[c], recv_sem=core_recv.at[c], device_id=core_peer, device_id_type=MESH)

    def copy_y(c):
        return pltpu.make_async_remote_copy(
            src_ref=second.at[:, pl.ds(c * CS, CS), :], dst_ref=second_in.at[:, pl.ds(c * CS, CS), :],
            send_sem=y_send.at[c], recv_sem=y_recv.at[c], device_id=y_peer, device_id_type=MESH)

    def copy_own(c):
        return pltpu.make_async_copy(
            slots.at[pl.ds(me * CAP, CAP), pl.ds(c * CS, CS), :],
            out_ref.at[pl.ds(me * CAP, CAP), pl.ds(c * CS, CS), :], own_sem.at[c])

    sign = pair_sign(CS)

    def finish(c):
        lo = c * CS
        copy_y(c).wait_recv()

        def row(g, _):
            got = second_in[g, pl.ds(lo, CS), :]
            at = ROWS + g
            merged[g] = second[g, pl.ds(lo, CS), :] + got * turn_cos[at] + swapped(got) * (turn_sin[at] * sign)
            return 0
        lax.fori_loop(0, ROWS, row, 0)

        def slot(q, _):
            value = merged[slot_row[q]]
            slots[q, pl.ds(lo, CS), :] = jnp.where(slot_used[q] > 0, value, 0.0)
            return 0
        lax.fori_loop(0, BEAMS * CAP, slot, 0)

        def send(shift, _):
            to = me ^ shift
            pltpu.make_async_remote_copy(
                src_ref=slots.at[pl.ds(to * CAP, CAP), pl.ds(lo, CS), :],
                dst_ref=out_ref.at[pl.ds(me * CAP, CAP), pl.ds(lo, CS), :],
                send_sem=beam_send, recv_sem=beam_recv, device_id=(sub, to), device_id_type=MESH).start()
            return 0
        lax.fori_loop(1, BEAMS, send, 0)
        copy_own(c).start()

    project(0, 0)
    project(1, 0)
    for c in range(CHUNKS):
        lo = c * CS
        if c + 1 < CHUNKS:
            project(0, lo + CS)

        def row0(g, _, lo=lo):
            first[g, pl.ds(lo, CS), :] = sub_ref[g, pl.ds(lo, CS), :] + added(0, g, lo)
            return 0
        lax.fori_loop(0, ROWS, row0, 0)
        if c == 0:
            pl.semaphore_wait(barrier, BEAMS + 1)
        copy_core(c).start()
        if c + 1 < CHUNKS:
            project(1, lo + CS)

        def row1(g, _, lo=lo):
            late[g] = added(1, g, lo)
            return 0
        lax.fori_loop(0, ROWS, row1, 0)
        copy_core(c).wait_recv()

        def turn0(g, _, lo=lo):
            got = first_in[g, pl.ds(lo, CS), :]
            second[g, pl.ds(lo, CS), :] = (
                first[g, pl.ds(lo, CS), :] + late[g]
                + got * turn_cos[g] + swapped(got) * (turn_sin[g] * sign))
            return 0
        lax.fori_loop(0, ROWS, turn0, 0)
        copy_y(c).start()
        if c >= 1:
            finish(c - 1)
    finish(CHUNKS - 1)
    for c in range(CHUNKS):
        copy_core(c).wait_send()
        copy_y(c).wait_send()
        copy_own(c).wait()
    rest = slots.at[pl.ds(0, (BEAMS - 1) * CAP)]
    pltpu.make_async_copy(rest, rest, beam_send).wait()
    landed = out_ref.at[pl.ds(0, (BEAMS - 1) * CAP)]
    pltpu.make_async_copy(landed, landed, beam_recv).wait()


def merge_call(scalars, rows, got, cos_table, sin_table):
    smem = pl.BlockSpec(memory_space=pltpu.SMEM)
    vmem = pl.BlockSpec(memory_space=pltpu.VMEM)
    full = (ROWS, SUBL, LANES)
    return pl.pallas_call(
        merge_kernel,
        out_shape=jax.ShapeDtypeStruct((BEAMS * CAP, SUBL, LANES), jnp.float32),
        in_specs=[smem] * 9 + [vmem] * 4,
        out_specs=pl.BlockSpec(memory_space=pl.ANY),
        scratch_shapes=[
            pltpu.VMEM((2, ROWS, SUBL + PAD, LANES), jnp.float32),
            pltpu.VMEM(full, jnp.float32),
            pltpu.VMEM(full, jnp.float32),
            pltpu.VMEM((ROWS, CS, LANES), jnp.float32),
            pltpu.VMEM(full, jnp.float32),
            pltpu.VMEM(full, jnp.float32),
            pltpu.VMEM((ROWS, CS, LANES), jnp.float32),
            pltpu.VMEM((BEAMS * CAP, SUBL, LANES), jnp.float32),
            pltpu.SemaphoreType.DMA((CHUNKS,)),
            pltpu.SemaphoreType.DMA((CHUNKS,)),
            pltpu.SemaphoreType.DMA((CHUNKS,)),
            pltpu.SemaphoreType.DMA((CHUNKS,)),
            pltpu.SemaphoreType.DMA,
            pltpu.SemaphoreType.DMA,
            pltpu.SemaphoreType.DMA((CHUNKS,)),
        ],
        compiler_params=pltpu.CompilerParams(
            collective_id=1, has_side_effects=True, vmem_limit_bytes=48 * 2**20
        ),
    )(*scalars, rows, got, cos_table, sin_table)


def paired(x):
    lead = x.shape[:-2]
    n = len(lead)
    y = x.reshape(*lead, 2, SUBL // 2, LANES)
    y = y.transpose(*range(n), n + 1, n, n + 2)
    return y.reshape(*lead, SUBL, LANES)


def ramp_tables(cycles):
    length = SUBL // 2 * LANES
    scale = TWO_PI / length
    blocks = jnp.arange(SUBL // 8, dtype=jnp.int32) * (4 * LANES)
    coarse = (cycles[:, :, None] * blocks % length).astype(jnp.float32) * scale
    place = (
        jnp.arange(8, dtype=jnp.int32)[:, None] // 2 * LANES
        + jnp.arange(LANES, dtype=jnp.int32)[None, :]
    )
    fine = (cycles[:, :, None, None] * place % length).astype(jnp.float32) * scale
    return jnp.cos(coarse), jnp.sin(coarse), jnp.cos(fine), jnp.sin(fine)


def per_device(
    subimage, pulses, ingest_owner, weights, offsets, filter_taps, cycles, merge_phase, destination
):
    me = lax.axis_index("beam")
    mine = (ingest_owner[:, 0] == me)[:, None, None, None]
    block = paired(pulses[:, 0, 0])
    got = lax.psum(jnp.where(mine, block, 0.0), "beam")
    coarse_cos, coarse_sin, fine_cos, fine_sin = ramp_tables(cycles[:, 0])
    targets = destination[:, 0]
    same_owner = targets[:, None] == targets[None, :]
    order = jnp.arange(ROWS, dtype=jnp.int32)
    rank = jnp.sum((same_owner & (order[None, :] < order[:, None])).astype(jnp.int32), axis=1)
    table = jnp.arange(BEAMS * CAP, dtype=jnp.int32)[:, None] == (targets * CAP + rank)[None, :]
    slot_row = jnp.sum(jnp.where(table, order[None, :], 0), axis=1)
    slot_used = jnp.sum(table.astype(jnp.int32), axis=1)
    scalars = (
        weights[:, 0].reshape(-1),
        offsets[:, 0].reshape(-1),
        filter_taps[:, 0].reshape(-1),
        coarse_cos.reshape(-1),
        coarse_sin.reshape(-1),
        jnp.cos(merge_phase[:, 0]).reshape(-1),
        jnp.sin(merge_phase[:, 0]).reshape(-1),
        slot_row,
        slot_used,
    )
    out = merge_call(scalars, paired(subimage[0]), got, fine_cos, fine_sin)
    out = out.reshape(BEAMS * CAP, SUBL // 2, 2, LANES).transpose(0, 2, 1, 3)
    return out.reshape(1, BEAMS * CAP, 2, SUBL // 2 * LANES)


def solution(mesh):
    in_specs = (
        P("sub", "beam", None, None),
        P(None, "sub", "beam", None, None, None),
        P(None, "sub"),
        P(None, "sub", "beam", None, None),
        P(None, "sub", "beam"),
        P(None, "sub", "beam", None),
        P(None, "sub", "beam"),
        P(None, "sub", "beam"),
        P("beam", None),
    )
    out_specs = P("sub", "beam", None, None)
    return jax.shard_map(
        per_device, mesh=mesh, in_specs=in_specs, out_specs=out_specs, check_vma=False
    )
```

```python
import functools
import math

import jax
import jax.numpy as jnp
import numpy as np
from jax import lax
from jax.experimental import pallas as pl
from jax.experimental.pallas import tpu as pltpu
from jax.sharding import PartitionSpec as P

CAP = 2
TAPS = 8
PB = 16
ROWS = 16
BEAMS = 16
LANES = 128
SUBL = 256
PAD = 32
CHUNKS = 8
CS = SUBL // CHUNKS
TWO_PI = 2.0 * math.pi
MESH = pl.DeviceIdType.MESH


def swapped(x):
    n = x.shape[0] // 8
    y = x.reshape(n, 8, LANES)
    even = lax.broadcasted_iota(jnp.int32, (n, 8, LANES), 1) % 2 == 0
    z = jnp.where(even, pltpu.roll(y, 7, 1), pltpu.roll(y, 1, 1))
    return z.reshape(x.shape)


def pair_sign(rows):
    even = lax.broadcasted_iota(jnp.int32, (rows, LANES), 0) % 2 == 0
    return jnp.where(even, -1.0, 1.0).astype(jnp.float32)


def merge_kernel(
    weights, offsets, taps, block_cos, block_sin, turn_cos, turn_sin, slot_row, slot_used,
    sub_ref, got_ref, cos_ref, sin_ref,
    out_ref,
    proj, first, first_in, late, second, second_in, merged, slots,
    core_send, core_recv, y_send, y_recv, beam_send, beam_recv, own_sem,
):
    sub = lax.axis_index("sub")
    me = lax.axis_index("beam")
    core_peer = (sub ^ 1, me)
    y_peer = (sub ^ 2, me)

    barrier = pltpu.get_barrier_semaphore()
    pl.semaphore_signal(barrier, inc=1, device_id=core_peer, device_id_type=MESH)
    pl.semaphore_signal(barrier, inc=1, device_id=y_peer, device_id_type=MESH)
    for shift in range(1, BEAMS):
        pl.semaphore_signal(barrier, inc=1, device_id=(sub, me ^ shift), device_id_type=MESH)

    zero = jnp.zeros((PAD, LANES), jnp.float32)
    for s in range(2):
        def clear(g, _, s=s):
            proj[s, g, pl.ds(SUBL, PAD), :] = zero
            return 0
        lax.fori_loop(0, ROWS, clear, 0)

    def project(s, lo):
        def half(h, _):
            acc = [None] * 8
            for p in range(PB):
                b = got_ref[s, p, pl.ds(lo, CS), :]
                t = swapped(b) * pair_sign(CS)
                for k in range(8):
                    at = ((s * ROWS) + h * 8 + k) * 32 + p
                    term = weights[at] * b + weights[at + 16] * t
                    acc[k] = term if acc[k] is None else acc[k] + term
            for k in range(8):
                proj[s, h * 8 + k, pl.ds(lo, CS), :] = acc[k]
            return 0
        lax.fori_loop(0, 2, half, 0)

    lane = lax.broadcasted_iota(jnp.int32, (CS, LANES), 1)
    lane_w = lax.broadcasted_iota(jnp.int32, (CS + 8, LANES), 1)

    def added(s, g, lo):
        off = offsets[s * ROWS + g]
        a = off // LANES
        b = off % LANES
        v = proj[s, g, pl.ds(lo + 2 * a, CS + 8), :]
        u = pltpu.roll(v, lax.rem(LANES - b, LANES), 1)
        up = jnp.concatenate([u[2:], u[:2]], axis=0)
        w = jnp.where(lane_w < LANES - b, u, up)
        here, following = w[:CS], w[2 : CS + 2]
        base = (s * ROWS + g) * TAPS
        acc = taps[base] * here
        for k in range(1, TAPS):
            acc = acc + taps[base + k] * pltpu.roll(jnp.where(lane < k, following, here), LANES - k, 1)
        c0 = cos_ref[s, g]
        s0 = sin_ref[s, g]
        sign = pair_sign(8)
        parts = []
        turned = swapped(acc)
        for v8 in range(CS // 8):
            at = (s * ROWS + g) * (SUBL // 8) + lo // 8 + v8
            ci = block_cos[at]
            si = block_sin[at]
            cc = c0 * ci - s0 * si
            ss = (s0 * ci + c0 * si) * sign
            parts.append(acc[v8 * 8 : v8 * 8 + 8] * cc + turned[v8 * 8 : v8 * 8 + 8] * ss)
        return jnp.concatenate(parts, axis=0)

    def copy_core(c):
        return pltpu.make_async_remote_copy(
            src_ref=first.at[:, pl.ds(c * CS, CS), :], dst_ref=first_in.at[:, pl.ds(c * CS, CS), :],
            send_sem=core_send.at[c], recv_sem=core_recv.at[c], device_id=core_peer, device_id_type=MESH)

    def copy_y(c):
        return pltpu.make_async_remote_copy(
            src_ref=second.at[:, pl.ds(c * CS, CS), :], dst_ref=second_in.at[:, pl.ds(c * CS, CS), :],
            send_sem=y_send.at[c], recv_sem=y_recv.at[c], device_id=y_peer, device_id_type=MESH)

    def copy_own(c):
        return pltpu.make_async_copy(
            slots.at[pl.ds(me * CAP, CAP), pl.ds(c * CS, CS), :],
            out_ref.at[pl.ds(me * CAP, CAP), pl.ds(c * CS, CS), :], own_sem.at[c])

    sign = pair_sign(CS)

    def finish(c):
        lo = c * CS
        copy_y(c).wait_recv()

        def row(g, _):
            got = second_in[g, pl.ds(lo, CS), :]
            at = ROWS + g
            merged[g] = second[g, pl.ds(lo, CS), :] + got * turn_cos[at] + swapped(got) * (turn_sin[at] * sign)
            return 0
        lax.fori_loop(0, ROWS, row, 0)

        def slot(q, _):
            value = merged[slot_row[q]]
            slots[q, pl.ds(lo, CS), :] = jnp.where(slot_used[q] > 0, value, 0.0)
            return 0
        lax.fori_loop(0, BEAMS * CAP, slot, 0)

        def send(shift, _):
            to = me ^ shift
            pltpu.make_async_remote_copy(
                src_ref=slots.at[pl.ds(to * CAP, CAP), pl.ds(lo, CS), :],
                dst_ref=out_ref.at[pl.ds(me * CAP, CAP), pl.ds(lo, CS), :],
                send_sem=beam_send, recv_sem=beam_recv, device_id=(sub, to), device_id_type=MESH).start()
            return 0
        lax.fori_loop(1, BEAMS, send, 0)
        copy_own(c).start()

    def start_core(c):
        lo = c * CS
        if c + 1 < CHUNKS:
            project(0, lo + CS)

        def row0(g, _):
            first[g, pl.ds(lo, CS), :] = sub_ref[g, pl.ds(lo, CS), :] + added(0, g, lo)
            return 0
        lax.fori_loop(0, ROWS, row0, 0)
        if c == 0:
            pl.semaphore_wait(barrier, BEAMS + 1)
        copy_core(c).start()

    def start_y(c):
        lo = c * CS
        if c + 1 < CHUNKS:
            project(1, lo + CS)

        def row1(g, _):
            late[g] = added(1, g, lo)
            return 0
        lax.fori_loop(0, ROWS, row1, 0)
        copy_core(c).wait_recv()

        def turn0(g, _):
            got = first_in[g, pl.ds(lo, CS), :]
            second[g, pl.ds(lo, CS), :] = (
                first[g, pl.ds(lo, CS), :] + late[g]
                + got * turn_cos[g] + swapped(got) * (turn_sin[g] * sign))
            return 0
        lax.fori_loop(0, ROWS, turn0, 0)
        copy_y(c).start()

    project(0, 0)
    project(1, 0)
    start_core(0)
    for c in range(CHUNKS):
        if c + 1 < CHUNKS:
            start_core(c + 1)
        start_y(c)
    for c in range(CHUNKS - 1):
        finish(c)
    finish(CHUNKS - 1)
    for c in range(CHUNKS):
        copy_core(c).wait_send()
        copy_y(c).wait_send()
        copy_own(c).wait()
    rest = slots.at[pl.ds(0, (BEAMS - 1) * CAP)]
    pltpu.make_async_copy(rest, rest, beam_send).wait()
    landed = out_ref.at[pl.ds(0, (BEAMS - 1) * CAP)]
    pltpu.make_async_copy(landed, landed, beam_recv).wait()


STEP = ((1, 0), (0, 1), (-1, 0), (0, -1))
TREE = {
    (0, 1): (1, 1), (0, 2): (1, 2), (0, 3): (1, 3), (1, 0): (3, 3), (1, 1): (0, 2), (1, 2): (0, 3),
    (1, 3): (1, 4), (2, 0): (3, 4), (2, 1): (2, 3), (2, 2): (0, 4), (2, 3): (1, 5), (3, 0): (3, 3),
    (3, 1): (2, 2), (3, 2): (1, 3), (3, 3): (1, 4),
}
DEPTH = 5
PARTS = 8
PS = SUBL // PARTS
STEPS = PARTS + DEPTH - 1


def tree_table():
    arrive = {}
    for (x, z), (way, hops) in TREE.items():
        for r in range(4):
            arrive[(x, z), r] = ((way + r) % 4, hops)
            x, z = -z % 4, x
    table = np.zeros((16, 12), np.int32)
    for x in range(4):
        for z in range(4):
            for e in range(4):
                there = ((x + STEP[e][0]) % 4, (z + STEP[e][1]) % 4)
                for r in range(4):
                    if (x, z) != (0, 0) and there != (0, 0) and arrive[there, r][0] == e:
                        table[x * 4 + z, e] = arrive[(x, z), r][0]
            for r in range(4):
                if (x, z) != (0, 0):
                    table[x * 4 + z, 4 + r] = arrive[(x, z), r][0]
                    table[x * 4 + z, 8 + r] = arrive[(x, z), r][1] - 1
    return table.reshape(-1)


def ingest_kernel(owner, table, block_ref, got_ref, *scratch):
    landing = [scratch[s * STEPS : (s + 1) * STEPS] for s in range(2)]
    stage, send_sem, recv_sem = scratch[2 * STEPS :]
    sub = lax.axis_index("sub")
    me = lax.axis_index("beam")
    x, z = me // 4, me % 4
    peers = [(sub, (x + dx + 4) % 4 * 4 + (z + dz + 4) % 4) for dx, dz in STEP]
    barrier = pltpu.get_barrier_semaphore()
    for peer in peers:
        pl.semaphore_signal(barrier, inc=1, device_id=peer, device_id_type=MESH)
    place = []
    for s in range(2):
        o = owner[s]
        place.append((((x - o // 4) & 3) * 4 + ((z - o % 4) & 3)) * 12)
    root = [place[s] == 0 for s in range(2)]
    pl.semaphore_wait(barrier, 4)

    for t in range(STEPS):
        for s in range(2):
            if t > 0:
                last = landing[s][t - 1]
                pltpu.make_async_copy(last, last, recv_sem.at[s, t - 1]).wait()
            for e in range(4):
                q = (e + 3) % 4
                if t < PARTS:
                    own = block_ref.at[s, pl.ds(4 * q, 4), pl.ds(t * PS, PS), :]
                if t == 0:
                    source = own
                else:
                    value = last[table[place[s] + e]]
                    if t < PARTS:
                        value = jnp.where(root[s], own[...], value)
                    source = stage.at[s, t - 1, e]
                    source[...] = value
                pltpu.make_async_remote_copy(
                    src_ref=source, dst_ref=landing[s][t].at[e], send_sem=send_sem, recv_sem=recv_sem.at[s, t],
                    device_id=peers[e], device_id_type=MESH).start()
    for s in range(2):
        last = landing[s][STEPS - 1]
        pltpu.make_async_copy(last, last, recv_sem.at[s, STEPS - 1]).wait()
    for s in range(2):
        for r in range(4):
            way = table[place[s] + 4 + r]
            late = table[place[s] + 8 + r]
            for c in range(PARTS):
                own = block_ref[s, pl.ds(4 * r, 4), pl.ds(c * PS, PS), :]
                value = landing[s][c][way]
                for d in range(1, DEPTH):
                    value = jnp.where(late == d, landing[s][c + d][way], value)
                got_ref[s, pl.ds(4 * r, 4), pl.ds(c * PS, PS), :] = jnp.where(root[s], own, value)
    for s in range(2):
        own = block_ref.at[s, :, pl.ds(0, PS), :]
        pltpu.make_async_copy(own, own, send_sem).wait()
        pltpu.make_async_copy(stage.at[s], stage.at[s], send_sem).wait()


def ingest(owner, blocks):
    smem = pl.BlockSpec(memory_space=pltpu.SMEM)
    vmem = pl.BlockSpec(memory_space=pltpu.VMEM)
    part = pltpu.VMEM((4, 4, PS, LANES), jnp.float32)
    return pl.pallas_call(
        ingest_kernel,
        out_shape=jax.ShapeDtypeStruct((2, PB, SUBL, LANES), jnp.float32),
        in_specs=[smem, smem, vmem],
        out_specs=vmem,
        scratch_shapes=[part] * (2 * STEPS) + [
            pltpu.VMEM((2, STEPS - 1, 4, 4, PS, LANES), jnp.float32),
            pltpu.SemaphoreType.DMA,
            pltpu.SemaphoreType.DMA((2, STEPS)),
        ],
        compiler_params=pltpu.CompilerParams(
            collective_id=2, has_side_effects=True, vmem_limit_bytes=32 * 2**20
        ),
    )(owner, jnp.asarray(tree_table()), blocks)


def merge_call(scalars, rows, got, cos_table, sin_table):
    smem = pl.BlockSpec(memory_space=pltpu.SMEM)
    vmem = pl.BlockSpec(memory_space=pltpu.VMEM)
    full = (ROWS, SUBL, LANES)
    return pl.pallas_call(
        merge_kernel,
        out_shape=jax.ShapeDtypeStruct((BEAMS * CAP, SUBL, LANES), jnp.float32),
        in_specs=[smem] * 9 + [vmem] * 4,
        out_specs=pl.BlockSpec(memory_space=pl.ANY),
        scratch_shapes=[
            pltpu.VMEM((2, ROWS, SUBL + PAD, LANES), jnp.float32),
            pltpu.VMEM(full, jnp.float32),
            pltpu.VMEM(full, jnp.float32),
            pltpu.VMEM((ROWS, CS, LANES), jnp.float32),
            pltpu.VMEM(full, jnp.float32),
            pltpu.VMEM(full, jnp.float32),
            pltpu.VMEM((ROWS, CS, LANES), jnp.float32),
            pltpu.VMEM((BEAMS * CAP, SUBL, LANES), jnp.float32),
            pltpu.SemaphoreType.DMA((CHUNKS,)),
            pltpu.SemaphoreType.DMA((CHUNKS,)),
            pltpu.SemaphoreType.DMA((CHUNKS,)),
            pltpu.SemaphoreType.DMA((CHUNKS,)),
            pltpu.SemaphoreType.DMA,
            pltpu.SemaphoreType.DMA,
            pltpu.SemaphoreType.DMA((CHUNKS,)),
        ],
        compiler_params=pltpu.CompilerParams(
            collective_id=1, has_side_effects=True, vmem_limit_bytes=48 * 2**20
        ),
    )(*scalars, rows, got, cos_table, sin_table)


def paired(x):
    lead = x.shape[:-2]
    n = len(lead)
    y = x.reshape(*lead, 2, SUBL // 2, LANES)
    y = y.transpose(*range(n), n + 1, n, n + 2)
    return y.reshape(*lead, SUBL, LANES)


def ramp_tables(cycles):
    length = SUBL // 2 * LANES
    scale = TWO_PI / length
    blocks = jnp.arange(SUBL // 8, dtype=jnp.int32) * (4 * LANES)
    coarse = (cycles[:, :, None] * blocks % length).astype(jnp.float32) * scale
    place = (
        jnp.arange(8, dtype=jnp.int32)[:, None] // 2 * LANES
        + jnp.arange(LANES, dtype=jnp.int32)[None, :]
    )
    fine = (cycles[:, :, None, None] * place % length).astype(jnp.float32) * scale
    return jnp.cos(coarse), jnp.sin(coarse), jnp.cos(fine), jnp.sin(fine)


def per_device(
    subimage, pulses, ingest_owner, weights, offsets, filter_taps, cycles, merge_phase, destination
):
    got = ingest(ingest_owner[:, 0], paired(pulses[:, 0, 0]))
    coarse_cos, coarse_sin, fine_cos, fine_sin = ramp_tables(cycles[:, 0])
    targets = destination[:, 0]
    same_owner = targets[:, None] == targets[None, :]
    order = jnp.arange(ROWS, dtype=jnp.int32)
    rank = jnp.sum((same_owner & (order[None, :] < order[:, None])).astype(jnp.int32), axis=1)
    table = jnp.arange(BEAMS * CAP, dtype=jnp.int32)[:, None] == (targets * CAP + rank)[None, :]
    slot_row = jnp.sum(jnp.where(table, order[None, :], 0), axis=1)
    slot_used = jnp.sum(table.astype(jnp.int32), axis=1)
    scalars = (
        weights[:, 0].reshape(-1),
        offsets[:, 0].reshape(-1),
        filter_taps[:, 0].reshape(-1),
        coarse_cos.reshape(-1),
        coarse_sin.reshape(-1),
        jnp.cos(merge_phase[:, 0]).reshape(-1),
        jnp.sin(merge_phase[:, 0]).reshape(-1),
        slot_row,
        slot_used,
    )
    out = merge_call(scalars, paired(subimage[0]), got, fine_cos, fine_sin)
    out = out.reshape(BEAMS * CAP, SUBL // 2, 2, LANES).transpose(0, 2, 1, 3)
    return out.reshape(1, BEAMS * CAP, 2, SUBL // 2 * LANES)


def solution(mesh):
    in_specs = (
        P("sub", "beam", None, None),
        P(None, "sub", "beam", None, None, None),
        P(None, "sub"),
        P(None, "sub", "beam", None, None),
        P(None, "sub", "beam"),
        P(None, "sub", "beam", None),
        P(None, "sub", "beam"),
        P(None, "sub", "beam"),
        P("beam", None),
    )
    out_specs = P("sub", "beam", None, None)
    return jax.shard_map(
        per_device, mesh=mesh, in_specs=in_specs, out_specs=out_specs, check_vma=False
    )
```

```python
import math

import jax
import jax.numpy as jnp
import numpy as np
from jax import lax
from jax.experimental import pallas as pl
from jax.experimental.pallas import tpu as pltpu
from jax.sharding import PartitionSpec as P

CAP = 2
TAPS = 8
PB = 16
ROWS = 16
BEAMS = 16
SLOTS = BEAMS * CAP
LANES = 128
LENGTH = 16384
SUBL = 256
PAD = 32
MESH = pl.DeviceIdType.MESH

STEP = ((1, 0), (0, 1), (-1, 0), (0, -1))
TREE = {
    (0, 1): (1, 1), (0, 2): (1, 2), (0, 3): (1, 3), (1, 0): (3, 3), (1, 1): (0, 2), (1, 2): (0, 3),
    (1, 3): (1, 4), (2, 0): (3, 4), (2, 1): (2, 3), (2, 2): (0, 4), (2, 3): (1, 5), (3, 0): (3, 3),
    (3, 1): (2, 2), (3, 2): (1, 3), (3, 3): (1, 4),
}
DEPTH = 5
PARTS = 8
PS = SUBL // PARTS
STEPS = PARTS + DEPTH - 1
HALO = 16
BOUNDS = [0] + [PS * i - HALO for i in range(1, PARTS + 1)] + [SUBL]
CHUNKS = PARTS + 1
WINDOW = 2


def tree_table():
    arrive = {}
    for (x, z), (way, hops) in TREE.items():
        for r in range(4):
            arrive[(x, z), r] = ((way + r) % 4, hops)
            x, z = -z % 4, x
    table = np.zeros((16, 12), np.int32)
    for x in range(4):
        for z in range(4):
            for e in range(4):
                there = ((x + STEP[e][0]) % 4, (z + STEP[e][1]) % 4)
                for r in range(4):
                    if (x, z) != (0, 0) and there != (0, 0) and arrive[there, r][0] == e:
                        table[x * 4 + z, e] = arrive[(x, z), r][0]
            for r in range(4):
                if (x, z) != (0, 0):
                    table[x * 4 + z, 4 + r] = arrive[(x, z), r][0]
                    table[x * 4 + z, 8 + r] = arrive[(x, z), r][1] - 1
    return table.reshape(-1)


def swapped(x):
    shape = x.shape
    y = x.reshape(-1, 8, LANES)
    even = lax.broadcasted_iota(jnp.int32, y.shape, 1) % 2 == 0
    return jnp.where(even, pltpu.roll(y, 7, 1), pltpu.roll(y, 1, 1)).reshape(shape)


def pair_sign(rows):
    even = lax.broadcasted_iota(jnp.int32, (rows, LANES), 0) % 2 == 0
    return jnp.where(even, -1.0, 1.0).astype(jnp.float32)


def turn(n):
    quarter = (n + LENGTH // 8) // (LENGTH // 4)
    x = (n - quarter * (LENGTH // 4)).astype(jnp.float32) * (2.0 * math.pi / LENGTH)
    q = x * x
    c = 1.0 + q * (-1.0 / 2 + q * (1.0 / 24 + q * (-1.0 / 720 + q * (1.0 / 40320))))
    s = x * (1.0 + q * (-1.0 / 6 + q * (1.0 / 120 + q * (-1.0 / 5040 + q * (1.0 / 362880)))))
    odd = quarter % 2 == 1
    half = quarter % 4
    cos = jnp.where(odd, s, c) * jnp.where((half == 1) | (half == 2), -1.0, 1.0)
    sin = jnp.where(odd, c, s) * jnp.where(half >= 2, -1.0, 1.0)
    return cos, sin


def kernel(
    owner, weights, offsets, taps, cycles, phases, targets, table,
    sub_hbm, pulse_hbm,
    out_ref,
    *scratch,
):
    landing = [scratch[s * STEPS : (s + 1) * STEPS] for s in range(2)]
    (stage, sub_ref, block_ref, got, got_turned, proj, shifted, ramped, ramp_cos, ramp_sin, step_cos, step_sin,
     turn_cos, turn_sin, first, first_in, second, second_in, merged, slots, slot_row,
     load_sem, part_send, part_recv, core_send, core_recv, y_send, y_recv, beam_send, beam_recv, own_sem,
     ) = scratch[2 * STEPS :]
    sub = lax.axis_index("sub")
    me = lax.axis_index("beam")
    x, z = me // 4, me % 4
    core_peer = (sub ^ 1, me)
    y_peer = (sub ^ 2, me)
    peers = [(sub, (x + dx + 4) % 4 * 4 + (z + dz + 4) % 4) for dx, dz in STEP]

    barrier = pltpu.get_barrier_semaphore()
    pl.semaphore_signal(barrier, inc=1, device_id=core_peer, device_id_type=MESH)
    pl.semaphore_signal(barrier, inc=1, device_id=y_peer, device_id_type=MESH)
    for shift in range(1, BEAMS):
        pl.semaphore_signal(barrier, inc=1, device_id=(sub, me ^ shift), device_id_type=MESH)

    loads = [pltpu.make_async_copy(pulse_hbm, block_ref, load_sem.at[0]),
             pltpu.make_async_copy(sub_hbm, sub_ref, load_sem.at[1])]
    for load in loads:
        load.start()

    place = []
    for s in range(2):
        o = owner[s, 0]
        place.append((((x - o // 4) & 3) * 4 + ((z - o % 4) & 3)) * 12)
    root = [place[s] == 0 for s in range(2)]

    def prepare_rows(s, lo, hi):
        sublane = lax.broadcasted_iota(jnp.int32, (8, LANES), 0)
        place_in = sublane // 2 * LANES + lax.broadcasted_iota(jnp.int32, (8, LANES), 1)
        sign = pair_sign(8)

        def prepare(g, _):
            count = cycles[s, 0, g]
            cos, sin = turn((place_in * count) % LENGTH)
            ramp_cos[s, g] = cos
            ramp_sin[s, g] = sin * sign
            whole = jnp.full((8, LANES), (count * (4 * LANES)) % LENGTH, jnp.int32)
            cos, sin = turn(whole)
            step_cos[s, g] = cos
            step_sin[s, g] = sin * sign
            phase = jnp.full((8, LANES), phases[s, 0, g], jnp.float32)
            turn_cos[s, g] = jnp.cos(phase)
            turn_sin[s, g] = jnp.sin(phase) * sign
            return 0
        lax.fori_loop(lo, hi, prepare, 0)

    def prepare_slots():
        def one(o, _):
            low, high = jnp.int32(ROWS), jnp.int32(ROWS)
            for g in reversed(range(ROWS)):
                hit = targets[g, 0] == o
                high = jnp.where(hit, low, high)
                low = jnp.where(hit, g, low)
            slot_row[CAP * o] = low
            slot_row[CAP * o + 1] = high
            return 0
        lax.fori_loop(0, BEAMS, one, 0)

        def clear(g, _):
            for s in range(2):
                proj[s, g, pl.ds(SUBL, PAD), :] = jnp.zeros((PAD, LANES), jnp.float32)
            return 0
        lax.fori_loop(0, ROWS, clear, 0)

    def forward(s, t):
        if t > 0:
            last = landing[s][t - 1]
            pltpu.make_async_copy(last, last, part_recv.at[s, t - 1]).wait()
        if t == STEPS:
            return
        for e in range(4):
            q = (e + 3) % 4
            if t < PARTS:
                own = block_ref.at[s, pl.ds(4 * q, 4), pl.ds(t * PS, PS), :]
            if t == 0:
                source = own
            else:
                value = last[table[place[s] + e]]
                if t < PARTS:
                    value = jnp.where(root[s], own[...], value)
                source = stage.at[s, t - 1, e]
                source[...] = value
            pltpu.make_async_remote_copy(
                src_ref=source, dst_ref=landing[s][t].at[e], send_sem=part_send, recv_sem=part_recv.at[s, t],
                device_id=peers[e], device_id_type=MESH).start()

    def assemble(s, c):
        for r in range(4):
            way = table[place[s] + 4 + r]
            late = table[place[s] + 8 + r]
            for p in range(4):
                own = block_ref[s, 4 * r + p, pl.ds(c * PS, PS), :]
                value = landing[s][c][way, p]
                for d in range(1, DEPTH):
                    value = jnp.where(late == d, landing[s][c + d][way, p], value)
                value = jnp.where(root[s], own, value)
                got[4 * r + p] = value
                got_turned[4 * r + p] = swapped(value) * pair_sign(PS)

    def project(s, c):
        def half(h, _):
            acc = [None] * 8
            for p in range(PB):
                b = got[p]
                t = got_turned[p]
                for k in range(8):
                    g = h * 8 + k
                    term = weights[s, 0, g, 0, p] * b + weights[s, 0, g, 1, p] * t
                    acc[k] = term if acc[k] is None else acc[k] + term
            for k in range(8):
                g = h * 8 + k
                off = offsets[s, 0, g] % LANES
                proj[s, g, pl.ds(c * PS, PS), :] = pltpu.roll(acc[k], (LANES - off) % LANES, 1)
            return 0
        lax.fori_loop(0, 2, half, 0)

    def added(s, g, k):
        lo, n = BOUNDS[k], BOUNDS[k + 1] - BOUNDS[k]
        wide = n + 8
        lane = lax.broadcasted_iota(jnp.int32, (wide, LANES), 1)
        off = offsets[s, 0, g]
        start = lo + 2 * (off // LANES)
        inside = lane < LANES - off % LANES
        u0 = proj[s, g, pl.ds(start, wide), :]
        u1 = proj[s, g, pl.ds(start + 2, wide), :]
        u2 = proj[s, g, pl.ds(start + 4, wide), :]
        here = jnp.where(inside, u0, u1)
        following = jnp.where(inside, u1, u2)
        moved = [here]
        for i in range(1, 4):
            moved.append(pltpu.roll(jnp.where(lane < i, following, here), LANES - i, 1))
        near = taps[s, 0, g, 0] * here[:n]
        far = taps[s, 0, g, 4] * here
        for i in range(1, 4):
            near = near + taps[s, 0, g, i] * moved[i][:n]
            far = far + taps[s, 0, g, 4 + i] * moved[i]
        shifted[g, pl.ds(0, wide), :] = far
        beyond = shifted[g, pl.ds(2, n), :]
        acc = near + pltpu.roll(jnp.where(lane[:n] < 4, beyond, far[:n]), LANES - 4, 1)
        ramped[g, pl.ds(8, n), :] = acc
        even = lax.broadcasted_iota(jnp.int32, (n, LANES), 0) % 2 == 0
        turned = jnp.where(even, ramped[g, pl.ds(9, n), :], ramped[g, pl.ds(7, n), :])
        cos, sin = ramp_cos[s, g], ramp_sin[s, g]
        cos_by, sin_by = step_cos[s, g], step_sin[s, g]
        parts = []
        for v in range(n // 8):
            parts.append(acc[v * 8 : v * 8 + 8] * cos + turned[v * 8 : v * 8 + 8] * sin)
            cos, sin = cos * cos_by - sin * sin_by, sin * cos_by + cos * sin_by
        ramp_cos[s, g] = cos
        ramp_sin[s, g] = sin
        return jnp.concatenate(parts, axis=0)

    def span(k):
        return pl.ds(BOUNDS[k], BOUNDS[k + 1] - BOUNDS[k])

    def copy_core(k):
        return pltpu.make_async_remote_copy(
            src_ref=first.at[:, span(k), :], dst_ref=first_in.at[:, span(k), :],
            send_sem=core_send.at[k], recv_sem=core_recv.at[k], device_id=core_peer, device_id_type=MESH)

    def copy_y(k):
        return pltpu.make_async_remote_copy(
            src_ref=second.at[:, span(k), :], dst_ref=second_in.at[:, span(k), :],
            send_sem=y_send.at[k], recv_sem=y_recv.at[k], device_id=y_peer, device_id_type=MESH)

    def copy_own(k):
        return pltpu.make_async_copy(
            slots.at[pl.ds(me * CAP, CAP), span(k), :], out_ref.at[pl.ds(me * CAP, CAP), span(k), :], own_sem.at[k])

    def rotated(value, s, g):
        n = value.shape[0] // 8
        y = value.reshape(n, 8, LANES)
        t = swapped(value).reshape(n, 8, LANES)
        return (y * turn_cos[s, g][None] + t * turn_sin[s, g][None]).reshape(value.shape)

    def begin(k):
        def row0(g, _):
            first[g, span(k), :] = sub_ref[g, span(k), :] + added(0, g, k)
            return 0
        lax.fori_loop(0, ROWS, row0, 0, unroll=4)
        copy_core(k).start()

    def extend(k):
        def row1(g, _):
            second[g, span(k), :] = first[g, span(k), :] + added(1, g, k)
            return 0
        lax.fori_loop(0, ROWS, row1, 0, unroll=4)

    def meet(k):
        copy_core(k).wait_recv()

        def row(g, _):
            second[g, span(k), :] = second[g, span(k), :] + rotated(first_in[g, span(k), :], 0, g)
            return 0
        lax.fori_loop(0, ROWS, row, 0, unroll=4)

    def finish(k):
        copy_y(k).wait_recv()
        if k + WINDOW < CHUNKS:
            copy_y(k + WINDOW).start()
        n = BOUNDS[k + 1] - BOUNDS[k]

        def row(g, _):
            merged[g, pl.ds(0, n), :] = second[g, span(k), :] + rotated(second_in[g, span(k), :], 1, g)
            return 0
        lax.fori_loop(0, ROWS, row, 0, unroll=4)

        def slot(q, _):
            g = slot_row[q]
            value = merged[jnp.minimum(g, ROWS - 1), pl.ds(0, n), :]
            slots[q, span(k), :] = jnp.where(g < ROWS, value, 0.0)
            return 0
        lax.fori_loop(0, SLOTS, slot, 0, unroll=8)

        def send(shift, _):
            to = me ^ shift
            pltpu.make_async_remote_copy(
                src_ref=slots.at[pl.ds(to * CAP, CAP), span(k), :],
                dst_ref=out_ref.at[pl.ds(me * CAP, CAP), span(k), :],
                send_sem=beam_send, recv_sem=beam_recv, device_id=(sub, to), device_id_type=MESH).start()
            return 0
        lax.fori_loop(1, BEAMS, send, 0)
        copy_own(k).start()

    pl.semaphore_wait(barrier, BEAMS + 1)
    for load in loads:
        load.wait()
    for t in range(STEPS + 1):
        for s in range(2):
            forward(s, t)
        if t < 4:
            prepare_rows(t // 2, t % 2 * 8, t % 2 * 8 + 8)
        if t == 4:
            prepare_slots()
        c = t - DEPTH
        if c >= 1:
            meet(c - 1)
            if c - 1 < WINDOW:
                copy_y(c - 1).start()
        if c >= 0:
            assemble(0, c)
            project(0, c)
            begin(c)
            assemble(1, c)
            project(1, c)
            extend(c)
    begin(CHUNKS - 1)
    extend(CHUNKS - 1)
    meet(CHUNKS - 2)
    meet(CHUNKS - 1)
    for k in range(CHUNKS):
        finish(k)

    for s in range(2):
        own = block_ref.at[s, :, pl.ds(0, PS), :]
        pltpu.make_async_copy(own, own, part_send).wait()
        pltpu.make_async_copy(stage.at[s], stage.at[s], part_send).wait()
    for k in range(CHUNKS):
        copy_core(k).wait_send()
        copy_y(k).wait_send()
        copy_own(k).wait()
    rest = slots.at[pl.ds(0, SLOTS - CAP)]
    pltpu.make_async_copy(rest, rest, beam_send).wait()
    landed = out_ref.at[pl.ds(0, SLOTS - CAP)]
    pltpu.make_async_copy(landed, landed, beam_recv).wait()


def call(*operands):
    smem = pl.BlockSpec(memory_space=pltpu.SMEM)
    hbm = pl.BlockSpec(memory_space=pl.ANY)

    def vmem(*shape):
        return pltpu.VMEM((*shape, LANES), jnp.float32)

    return pl.pallas_call(
        kernel,
        out_shape=jax.ShapeDtypeStruct((SLOTS, SUBL, LANES), jnp.float32),
        in_specs=[smem] * 8 + [hbm] * 2,
        out_specs=hbm,
        scratch_shapes=[vmem(4, 4, PS)] * (2 * STEPS) + [
            vmem(2, STEPS - 1, 4, 4, PS),
            vmem(ROWS, SUBL),
            vmem(2, PB, SUBL),
            vmem(PB, PS),
            vmem(PB, PS),
            vmem(2, ROWS, SUBL + PAD),
            vmem(ROWS, PS + 8),
            vmem(ROWS, PS + 16),
            vmem(2, ROWS, 8),
            vmem(2, ROWS, 8),
            vmem(2, ROWS, 8),
            vmem(2, ROWS, 8),
            vmem(2, ROWS, 8),
            vmem(2, ROWS, 8),
            vmem(ROWS, SUBL),
            vmem(ROWS, SUBL),
            vmem(ROWS, SUBL),
            vmem(ROWS, SUBL),
            vmem(ROWS, PS),
            vmem(SLOTS, SUBL),
            pltpu.SMEM((SLOTS,), jnp.int32),
            pltpu.SemaphoreType.DMA((2,)),
            pltpu.SemaphoreType.DMA,
            pltpu.SemaphoreType.DMA((2, STEPS)),
            pltpu.SemaphoreType.DMA((CHUNKS,)),
            pltpu.SemaphoreType.DMA((CHUNKS,)),
            pltpu.SemaphoreType.DMA((CHUNKS,)),
            pltpu.SemaphoreType.DMA((CHUNKS,)),
            pltpu.SemaphoreType.DMA,
            pltpu.SemaphoreType.DMA,
            pltpu.SemaphoreType.DMA((CHUNKS,)),
        ],
        compiler_params=pltpu.CompilerParams(
            collective_id=1, has_side_effects=True, vmem_limit_bytes=56 * 2**20
        ),
    )(*operands)


def paired(x):
    lead = x.shape[:-2]
    n = len(lead)
    y = x.reshape(*lead, 2, SUBL // 2, LANES)
    y = y.transpose(*range(n), n + 1, n, n + 2)
    return y.reshape(*lead, SUBL, LANES)


def per_device(
    subimage, pulses, ingest_owner, weights, offsets, filter_taps, cycles, merge_phase, destination
):
    out = call(
        ingest_owner, weights, offsets, filter_taps, cycles, merge_phase, destination, jnp.asarray(tree_table()),
        paired(subimage[0]), paired(pulses[:, 0, 0]),
    )
    out = out.reshape(SLOTS, SUBL // 2, 2, LANES).transpose(0, 2, 1, 3)
    return out.reshape(1, SLOTS, 2, LENGTH)


def solution(mesh):
    in_specs = (
        P("sub", "beam", None, None),
        P(None, "sub", "beam", None, None, None),
        P(None, "sub"),
        P(None, "sub", "beam", None, None),
        P(None, "sub", "beam"),
        P(None, "sub", "beam", None),
        P(None, "sub", "beam"),
        P(None, "sub", "beam"),
        P("beam", None),
    )
    out_specs = P("sub", "beam", None, None)
    return jax.shard_map(
        per_device, mesh=mesh, in_specs=in_specs, out_specs=out_specs, check_vma=False
    )
```

```python
import functools
import math

import jax
import jax.numpy as jnp
import numpy as np
from jax import lax
from jax.experimental import pallas as pl
from jax.experimental.pallas import tpu as pltpu
from jax.sharding import PartitionSpec as P

CAP = 2
TAPS = 8
PB = 16
ROWS = 16
BEAMS = 16
SLOTS = BEAMS * CAP
LANES = 128
LENGTH = 16384
SUBL = 256
PAD = 32
MESH = pl.DeviceIdType.MESH

STEP = ((1, 0), (0, 1), (-1, 0), (0, -1))
TREE = {
    (0, 1): (1, 1), (0, 2): (1, 2), (0, 3): (1, 3), (1, 0): (3, 3), (1, 1): (0, 2), (1, 2): (0, 3),
    (1, 3): (1, 4), (2, 0): (3, 4), (2, 1): (2, 3), (2, 2): (0, 4), (2, 3): (1, 5), (3, 0): (3, 3),
    (3, 1): (2, 2), (3, 2): (1, 3), (3, 3): (1, 4),
}
DEPTH = 5
PARTS = 8
PS = SUBL // PARTS
LINES = 4
LP = 4 // LINES
STEPS = PARTS + DEPTH - 1
HALO = 16
BOUNDS = [0] + [PS * i - HALO for i in range(1, PARTS + 1)] + [SUBL]
CHUNKS = PARTS + 1


def tree_table():
    arrive = {}
    for (x, z), (way, hops) in TREE.items():
        for r in range(4):
            arrive[(x, z), r] = ((way + r) % 4, hops)
            x, z = -z % 4, x
    table = np.zeros((16, 12), np.int32)
    for x in range(4):
        for z in range(4):
            for e in range(4):
                there = ((x + STEP[e][0]) % 4, (z + STEP[e][1]) % 4)
                for r in range(4):
                    if (x, z) != (0, 0) and there != (0, 0) and arrive[there, r][0] == e:
                        table[x * 4 + z, e] = arrive[(x, z), r][0]
            for r in range(4):
                if (x, z) != (0, 0):
                    table[x * 4 + z, 4 + r] = arrive[(x, z), r][0]
                    table[x * 4 + z, 8 + r] = arrive[(x, z), r][1] - 1
    return table.reshape(-1)


def swapped(x):
    shape = x.shape
    y = x.reshape(-1, 8, LANES)
    even = lax.broadcasted_iota(jnp.int32, y.shape, 1) % 2 == 0
    return jnp.where(even, pltpu.roll(y, 7, 1), pltpu.roll(y, 1, 1)).reshape(shape)


def pair_sign(rows):
    even = lax.broadcasted_iota(jnp.int32, (rows, LANES), 0) % 2 == 0
    return jnp.where(even, -1.0, 1.0).astype(jnp.float32)


def turn(n):
    quarter = (n + LENGTH // 8) // (LENGTH // 4)
    x = (n - quarter * (LENGTH // 4)).astype(jnp.float32) * (2.0 * math.pi / LENGTH)
    q = x * x
    c = 1.0 + q * (-1.0 / 2 + q * (1.0 / 24 + q * (-1.0 / 720 + q * (1.0 / 40320))))
    s = x * (1.0 + q * (-1.0 / 6 + q * (1.0 / 120 + q * (-1.0 / 5040 + q * (1.0 / 362880)))))
    odd = quarter % 2 == 1
    half = quarter % 4
    cos = jnp.where(odd, s, c) * jnp.where((half == 1) | (half == 2), -1.0, 1.0)
    sin = jnp.where(odd, c, s) * jnp.where(half >= 2, -1.0, 1.0)
    return cos, sin


def kernel(
    owner, weights, offsets, taps, cycles, phases, targets, table,
    sub_hbm, pulse_hbm,
    out_ref,
    *scratch,
):
    landing = [[scratch[(s * LINES + w) * STEPS : (s * LINES + w + 1) * STEPS] for w in range(LINES)] for s in range(2)]
    (stage, sub_ref, block_ref, got, got_turned, proj, shifted, ramped, ramp_cos, ramp_sin, step_cos, step_sin,
     turn_cos, turn_sin, first, first_in, second, second_in, merged, slots, slot_row,
     load_sem, part_send, part_recv, core_send, core_recv, y_send, y_recv, beam_send, beam_recv, own_sem,
     ) = scratch[2 * LINES * STEPS :]
    sub = lax.axis_index("sub")
    me = lax.axis_index("beam")
    x, z = me // 4, me % 4
    core_peer = (sub ^ 1, me)
    y_peer = (sub ^ 2, me)
    peers = [(sub, (x + dx + 4) % 4 * 4 + (z + dz + 4) % 4) for dx, dz in STEP]

    barrier = pltpu.get_barrier_semaphore()
    pl.semaphore_signal(barrier, inc=1, device_id=core_peer, device_id_type=MESH)
    pl.semaphore_signal(barrier, inc=1, device_id=y_peer, device_id_type=MESH)
    for shift in range(1, BEAMS):
        pl.semaphore_signal(barrier, inc=1, device_id=(sub, me ^ shift), device_id_type=MESH)

    loads = [pltpu.make_async_copy(pulse_hbm, block_ref, load_sem.at[0]),
             pltpu.make_async_copy(sub_hbm, sub_ref, load_sem.at[1])]
    for load in loads:
        load.start()

    place = []
    for s in range(2):
        o = owner[s]
        place.append((((x - o // 4) & 3) * 4 + ((z - o % 4) & 3)) * 12)
    root = [place[s] == 0 for s in range(2)]

    def prepare_rows(s, lo, hi):
        sublane = lax.broadcasted_iota(jnp.int32, (8, LANES), 0)
        place_in = sublane // 2 * LANES + lax.broadcasted_iota(jnp.int32, (8, LANES), 1)
        sign = pair_sign(8)

        def prepare(g, _):
            count = cycles[s, 0, g]
            cos, sin = turn((place_in * count) % LENGTH)
            ramp_cos[s, g] = cos
            ramp_sin[s, g] = sin * sign
            whole = jnp.full((8, LANES), (count * (4 * LANES)) % LENGTH, jnp.int32)
            cos, sin = turn(whole)
            step_cos[s, g] = cos
            step_sin[s, g] = sin * sign
            phase = jnp.full((8, LANES), phases[s, 0, g], jnp.float32)
            turn_cos[s, g] = jnp.cos(phase)
            turn_sin[s, g] = jnp.sin(phase) * sign
            return 0
        lax.fori_loop(lo, hi, prepare, 0)

    def prepare_slots():
        def one(o, _):
            low, high = jnp.int32(ROWS), jnp.int32(ROWS)
            for g in reversed(range(ROWS)):
                hit = targets[g] == o
                high = jnp.where(hit, low, high)
                low = jnp.where(hit, g, low)
            slot_row[CAP * o] = low
            slot_row[CAP * o + 1] = high
            return 0
        lax.fori_loop(0, BEAMS, one, 0)

        def clear(g, _):
            for s in range(2):
                proj[s, g, pl.ds(SUBL, PAD), :] = jnp.zeros((PAD, LANES), jnp.float32)
            return 0
        lax.fori_loop(0, ROWS, clear, 0)

    def forward(s, w, t):
        if t > 0:
            last = landing[s][w][t - 1]
            pltpu.make_async_copy(last, last, part_recv.at[s, w, t - 1]).wait()
        if t == STEPS:
            return
        for e in range(4):
            q = (e + 3) % 4
            if t < PARTS:
                own = block_ref.at[s, pl.ds(4 * q + LP * w, LP), pl.ds(t * PS, PS), :]
            if t == 0:
                source = own
            else:
                value = last[table[place[s] + e]]
                if t < PARTS:
                    value = jnp.where(root[s], own[...], value)
                source = stage.at[s, w, t - 1, e]
                source[...] = value
            pltpu.make_async_remote_copy(
                src_ref=source, dst_ref=landing[s][w][t].at[e], send_sem=part_send, recv_sem=part_recv.at[s, w, t],
                device_id=peers[e], device_id_type=MESH).start()

    def assemble(s, c):
        for r in range(4):
            way = table[place[s] + 4 + r]
            late = table[place[s] + 8 + r]
            for p in range(4):
                own = block_ref[s, 4 * r + p, pl.ds(c * PS, PS), :]
                value = landing[s][p // LP][c][way, p % LP]
                for d in range(1, DEPTH):
                    value = jnp.where(late == d, landing[s][p // LP][c + d][way, p % LP], value)
                value = jnp.where(root[s], own, value)
                got[4 * r + p] = value
                got_turned[4 * r + p] = swapped(value) * pair_sign(PS)

    def project(s, c):
        def half(h, _):
            acc = [None] * 8
            for p in range(PB):
                b = got[p]
                t = got_turned[p]
                for k in range(8):
                    g = h * 8 + k
                    term = weights[s, 0, g, 0, p] * b + weights[s, 0, g, 1, p] * t
                    acc[k] = term if acc[k] is None else acc[k] + term
            for k in range(8):
                g = h * 8 + k
                off = offsets[s, 0, g] % LANES
                proj[s, g, pl.ds(c * PS, PS), :] = pltpu.roll(acc[k], (LANES - off) % LANES, 1)
            return 0
        lax.fori_loop(0, 2, half, 0)

    def added(s, g, k):
        lo, n = BOUNDS[k], BOUNDS[k + 1] - BOUNDS[k]
        wide = n + 8
        lane = lax.broadcasted_iota(jnp.int32, (wide, LANES), 1)
        off = offsets[s, 0, g]
        start = lo + 2 * (off // LANES)
        inside = lane < LANES - off % LANES
        u0 = proj[s, g, pl.ds(start, wide), :]
        u1 = proj[s, g, pl.ds(start + 2, wide), :]
        u2 = proj[s, g, pl.ds(start + 4, wide), :]
        here = jnp.where(inside, u0, u1)
        following = jnp.where(inside, u1, u2)
        moved = [here]
        for i in range(1, 4):
            moved.append(pltpu.roll(jnp.where(lane < i, following, here), LANES - i, 1))
        near = taps[s, 0, 0, g] * here[:n]
        far = taps[s, 0, 4, g] * here
        for i in range(1, 4):
            near = near + taps[s, 0, i, g] * moved[i][:n]
            far = far + taps[s, 0, 4 + i, g] * moved[i]
        shifted[g, pl.ds(0, wide), :] = far
        beyond = shifted[g, pl.ds(2, n), :]
        acc = near + pltpu.roll(jnp.where(lane[:n] < 4, beyond, far[:n]), LANES - 4, 1)
        ramped[g, pl.ds(8, n), :] = acc
        even = lax.broadcasted_iota(jnp.int32, (n, LANES), 0) % 2 == 0
        turned = jnp.where(even, ramped[g, pl.ds(9, n), :], ramped[g, pl.ds(7, n), :])
        cos, sin = ramp_cos[s, g], ramp_sin[s, g]
        cos_by, sin_by = step_cos[s, g], step_sin[s, g]
        parts = []
        for v in range(n // 8):
            parts.append(acc[v * 8 : v * 8 + 8] * cos + turned[v * 8 : v * 8 + 8] * sin)
            cos, sin = cos * cos_by - sin * sin_by, sin * cos_by + cos * sin_by
        ramp_cos[s, g] = cos
        ramp_sin[s, g] = sin
        return jnp.concatenate(parts, axis=0)

    def span(k):
        return pl.ds(BOUNDS[k], BOUNDS[k + 1] - BOUNDS[k])

    def copy_core(k):
        return pltpu.make_async_remote_copy(
            src_ref=first.at[:, span(k), :], dst_ref=first_in.at[:, span(k), :],
            send_sem=core_send.at[k], recv_sem=core_recv.at[k], device_id=core_peer, device_id_type=MESH)

    def copy_y(k):
        return pltpu.make_async_remote_copy(
            src_ref=second.at[:, span(k), :], dst_ref=second_in.at[:, span(k), :],
            send_sem=y_send.at[k], recv_sem=y_recv.at[k], device_id=y_peer, device_id_type=MESH)

    def copy_own(k):
        return pltpu.make_async_copy(
            slots.at[pl.ds(me * CAP, CAP), span(k), :], out_ref.at[pl.ds(me * CAP, CAP), span(k), :], own_sem.at[k])

    def rotated(value, s, g):
        n = value.shape[0] // 8
        y = value.reshape(n, 8, LANES)
        t = swapped(value).reshape(n, 8, LANES)
        return (y * turn_cos[s, g][None] + t * turn_sin[s, g][None]).reshape(value.shape)

    def begin(k):
        def row0(g, _):
            first[g, span(k), :] = sub_ref[g, span(k), :] + added(0, g, k)
            return 0
        lax.fori_loop(0, ROWS, row0, 0, unroll=8)
        copy_core(k).start()

    def extend(k):
        def row1(g, _):
            second[g, span(k), :] = first[g, span(k), :] + added(1, g, k)
            return 0
        lax.fori_loop(0, ROWS, row1, 0, unroll=8)

    def meet(k):
        copy_core(k).wait_recv()

        def row(g, _):
            second[g, span(k), :] = second[g, span(k), :] + rotated(first_in[g, span(k), :], 0, g)
            return 0
        lax.fori_loop(0, ROWS, row, 0, unroll=4)
        copy_y(k).start()

    def finish(k):
        copy_y(k).wait_recv()
        n = BOUNDS[k + 1] - BOUNDS[k]

        def row(g, _):
            merged[g, pl.ds(0, n), :] = second[g, span(k), :] + rotated(second_in[g, span(k), :], 1, g)
            return 0
        lax.fori_loop(0, ROWS, row, 0, unroll=4)

        def slot(q, _):
            g = slot_row[q]
            value = merged[jnp.minimum(g, ROWS - 1), pl.ds(0, n), :]
            slots[q, span(k), :] = jnp.where(g < ROWS, value, 0.0)
            return 0
        lax.fori_loop(0, SLOTS, slot, 0, unroll=8)

        def send(shift, _):
            to = me ^ shift
            pltpu.make_async_remote_copy(
                src_ref=slots.at[pl.ds(to * CAP, CAP), span(k), :],
                dst_ref=out_ref.at[pl.ds(me * CAP, CAP), span(k), :],
                send_sem=beam_send, recv_sem=beam_recv, device_id=(sub, to), device_id_type=MESH).start()
            return 0
        lax.fori_loop(1, BEAMS, send, 0)
        copy_own(k).start()

    pl.semaphore_wait(barrier, BEAMS + 1)
    for load in loads:
        load.wait()
    def ready(s, k):
        assemble(s, k)
        project(s, k)

    def section0(k):
        if k < PARTS:
            ready(0, k)
        begin(k)

    def section1(k):
        if k < PARTS:
            ready(1, k)
        extend(k)

    early = (STEPS - DEPTH) // 2
    pieces = [functools.partial(prepare_rows, s, h * 8, h * 8 + 8) for s in range(2) for h in range(2)]
    pieces += [prepare_slots] + [None] * (2 * DEPTH - 5)
    for k in range(early + 1):
        pieces += [functools.partial(ready, 0, k), functools.partial(begin, k)]
        pieces += [functools.partial(ready, 1, k), functools.partial(extend, k)]
    for t in range(STEPS + 1):
        for s in range(2):
            for w in range(LINES):
                forward(s, w, t)
            k, odd = divmod(t - DEPTH, 2)
            if s == 0 and odd == 0 and 0 < k:
                meet(k - 1)
            if s == 0 and t == STEPS:
                finish(0)
            piece = pieces[2 * t + s]
            if piece is not None:
                piece()
    for piece in pieces[2 * STEPS + 2 :]:
        piece()
    finish(1)
    meet(early)
    for k in range(early + 1, CHUNKS):
        section0(k)
        finish(k - 2)
        section1(k)
        meet(k)
    finish(CHUNKS - 2)
    finish(CHUNKS - 1)

    for s in range(2):
        own = block_ref.at[s, :, pl.ds(0, PS), :]
        pltpu.make_async_copy(own, own, part_send).wait()
        pltpu.make_async_copy(stage.at[s], stage.at[s], part_send).wait()
    for k in range(CHUNKS):
        copy_core(k).wait_send()
        copy_y(k).wait_send()
        copy_own(k).wait()
    rest = slots.at[pl.ds(0, SLOTS - CAP)]
    pltpu.make_async_copy(rest, rest, beam_send).wait()
    landed = out_ref.at[pl.ds(0, SLOTS - CAP)]
    pltpu.make_async_copy(landed, landed, beam_recv).wait()


def call(*operands):
    smem = pl.BlockSpec(memory_space=pltpu.SMEM)
    hbm = pl.BlockSpec(memory_space=pl.ANY)

    def vmem(*shape):
        return pltpu.VMEM((*shape, LANES), jnp.float32)

    return pl.pallas_call(
        kernel,
        out_shape=jax.ShapeDtypeStruct((SLOTS, SUBL, LANES), jnp.float32),
        in_specs=[smem] * 8 + [hbm] * 2,
        out_specs=hbm,
        scratch_shapes=[vmem(4, LP, PS)] * (2 * LINES * STEPS) + [
            vmem(2, LINES, STEPS - 1, 4, LP, PS),
            vmem(ROWS, SUBL),
            vmem(2, PB, SUBL),
            vmem(PB, PS),
            vmem(PB, PS),
            vmem(2, ROWS, SUBL + PAD),
            vmem(ROWS, PS + 8),
            vmem(ROWS, PS + 16),
            vmem(2, ROWS, 8),
            vmem(2, ROWS, 8),
            vmem(2, ROWS, 8),
            vmem(2, ROWS, 8),
            vmem(2, ROWS, 8),
            vmem(2, ROWS, 8),
            vmem(ROWS, SUBL),
            vmem(ROWS, SUBL),
            vmem(ROWS, SUBL),
            vmem(ROWS, SUBL),
            vmem(ROWS, PS),
            vmem(SLOTS, SUBL),
            pltpu.SMEM((SLOTS,), jnp.int32),
            pltpu.SemaphoreType.DMA((2,)),
            pltpu.SemaphoreType.DMA,
            pltpu.SemaphoreType.DMA((2, LINES, STEPS)),
            pltpu.SemaphoreType.DMA((CHUNKS,)),
            pltpu.SemaphoreType.DMA((CHUNKS,)),
            pltpu.SemaphoreType.DMA((CHUNKS,)),
            pltpu.SemaphoreType.DMA((CHUNKS,)),
            pltpu.SemaphoreType.DMA,
            pltpu.SemaphoreType.DMA,
            pltpu.SemaphoreType.DMA((CHUNKS,)),
        ],
        compiler_params=pltpu.CompilerParams(
            collective_id=1, has_side_effects=True, vmem_limit_bytes=56 * 2**20
        ),
    )(*operands)


def paired(x):
    lead = x.shape[:-2]
    n = len(lead)
    y = x.reshape(*lead, 2, SUBL // 2, LANES)
    y = y.transpose(*range(n), n + 1, n, n + 2)
    return y.reshape(*lead, SUBL, LANES)


def per_device(
    subimage, pulses, ingest_owner, weights, offsets, filter_taps, cycles, merge_phase, destination
):
    out = call(
        ingest_owner[:, 0], weights, offsets, filter_taps.transpose(0, 1, 3, 2), cycles, merge_phase, destination[:, 0], jnp.asarray(tree_table()),
        paired(subimage[0]), paired(pulses[:, 0, 0]),
    )
    out = out.reshape(SLOTS, SUBL // 2, 2, LANES).transpose(0, 2, 1, 3)
    return out.reshape(1, SLOTS, 2, LENGTH)


def solution(mesh):
    in_specs = (
        P("sub", "beam", None, None),
        P(None, "sub", "beam", None, None, None),
        P(None, "sub"),
        P(None, "sub", "beam", None, None),
        P(None, "sub", "beam"),
        P(None, "sub", "beam", None),
        P(None, "sub", "beam"),
        P(None, "sub", "beam"),
        P("beam", None),
    )
    out_specs = P("sub", "beam", None, None)
    return jax.shard_map(
        per_device, mesh=mesh, in_specs=in_specs, out_specs=out_specs, check_vma=False
    )
```

```python
import functools
import math

import jax
import jax.numpy as jnp
import numpy as np
from jax import lax
from jax.experimental import pallas as pl
from jax.experimental.pallas import tpu as pltpu
from jax.sharding import PartitionSpec as P

CAP = 2
TAPS = 8
PB = 16
ROWS = 16
BEAMS = 16
SLOTS = BEAMS * CAP
LANES = 128
LENGTH = 16384
SUBL = 256
PAD = 32
MESH = pl.DeviceIdType.MESH

STEP = ((1, 0), (0, 1), (-1, 0), (0, -1))
TREE = {
    (0, 1): (1, 1), (0, 2): (1, 2), (0, 3): (1, 3), (1, 0): (3, 3), (1, 1): (0, 2), (1, 2): (0, 3),
    (1, 3): (1, 4), (2, 0): (3, 4), (2, 1): (2, 3), (2, 2): (0, 4), (2, 3): (1, 5), (3, 0): (3, 3),
    (3, 1): (2, 2), (3, 2): (1, 3), (3, 3): (1, 4),
}
DEPTH = 5
PARTS = 8
PS = SUBL // PARTS
LINES = 4
LP = 4 // LINES
STEPS = PARTS + DEPTH - 1
HALO = 16
BOUNDS = [0] + [PS * i - HALO for i in range(1, PARTS + 1)] + [SUBL]
CHUNKS = PARTS + 1
SMALL = 8


def tree_table():
    arrive = {}
    for (x, z), (way, hops) in TREE.items():
        for r in range(4):
            arrive[(x, z), r] = ((way + r) % 4, hops)
            x, z = -z % 4, x
    table = np.zeros((16, 12), np.int32)
    for x in range(4):
        for z in range(4):
            for e in range(4):
                there = ((x + STEP[e][0]) % 4, (z + STEP[e][1]) % 4)
                for r in range(4):
                    if (x, z) != (0, 0) and there != (0, 0) and arrive[there, r][0] == e:
                        table[x * 4 + z, e] = arrive[(x, z), r][0]
            for r in range(4):
                if (x, z) != (0, 0):
                    table[x * 4 + z, 4 + r] = arrive[(x, z), r][0]
                    table[x * 4 + z, 8 + r] = arrive[(x, z), r][1] - 1
    return table.reshape(-1)


def swapped(x):
    shape = x.shape
    y = x.reshape(-1, 8, LANES)
    even = lax.broadcasted_iota(jnp.int32, y.shape, 1) % 2 == 0
    return jnp.where(even, pltpu.roll(y, 7, 1), pltpu.roll(y, 1, 1)).reshape(shape)


def pair_sign(rows):
    even = lax.broadcasted_iota(jnp.int32, (rows, LANES), 0) % 2 == 0
    return jnp.where(even, -1.0, 1.0).astype(jnp.float32)


def turn(n):
    quarter = (n + LENGTH // 8) // (LENGTH // 4)
    x = (n - quarter * (LENGTH // 4)).astype(jnp.float32) * (2.0 * math.pi / LENGTH)
    q = x * x
    c = 1.0 + q * (-1.0 / 2 + q * (1.0 / 24 + q * (-1.0 / 720 + q * (1.0 / 40320))))
    s = x * (1.0 + q * (-1.0 / 6 + q * (1.0 / 120 + q * (-1.0 / 5040 + q * (1.0 / 362880)))))
    odd = quarter % 2 == 1
    half = quarter % 4
    cos = jnp.where(odd, s, c) * jnp.where((half == 1) | (half == 2), -1.0, 1.0)
    sin = jnp.where(odd, c, s) * jnp.where(half >= 2, -1.0, 1.0)
    return cos, sin


def kernel(*refs):
    small, (sub_hbm, pulse_hbm, out_ref), scratch = refs[:SMALL], refs[SMALL : SMALL + 3], refs[SMALL + 3 :]
    held, small_sem, scratch = scratch[:SMALL], scratch[SMALL], scratch[SMALL + 1 :]
    owner, weights, offsets, taps, cycles, phases, targets, table = held
    landing = [[scratch[(s * LINES + w) * STEPS : (s * LINES + w + 1) * STEPS] for w in range(LINES)] for s in range(2)]
    (stage, sub_ref, block_ref, got, got_turned, proj, shifted, ramped, ramp_cos, ramp_sin, step_cos, step_sin,
     turn_cos, turn_sin, first, first_in, second, second_in, merged, slots, slot_row,
     load_sem, part_send, part_recv, core_send, core_recv, y_send, y_recv, beam_send, beam_recv, own_sem,
     ) = scratch[2 * LINES * STEPS :]
    sub = lax.axis_index("sub")
    me = lax.axis_index("beam")
    x, z = me // 4, me % 4
    core_peer = (sub ^ 1, me)
    y_peer = (sub ^ 2, me)
    peers = [(sub, (x + dx + 4) % 4 * 4 + (z + dz + 4) % 4) for dx, dz in STEP]

    barrier = pltpu.get_barrier_semaphore()
    pl.semaphore_signal(barrier, inc=1, device_id=core_peer, device_id_type=MESH)
    pl.semaphore_signal(barrier, inc=1, device_id=y_peer, device_id_type=MESH)
    for shift in range(1, BEAMS):
        pl.semaphore_signal(barrier, inc=1, device_id=(sub, me ^ shift), device_id_type=MESH)

    fetches = [pltpu.make_async_copy(small[i], held[i], small_sem.at[i]) for i in range(SMALL)]
    for fetch in fetches:
        fetch.start()
    loads = [pltpu.make_async_copy(pulse_hbm, block_ref, load_sem.at[0]),
             pltpu.make_async_copy(sub_hbm, sub_ref, load_sem.at[1])]
    for load in loads:
        load.start()

    def prepare_rows(s, lo, hi):
        sublane = lax.broadcasted_iota(jnp.int32, (8, LANES), 0)
        place_in = sublane // 2 * LANES + lax.broadcasted_iota(jnp.int32, (8, LANES), 1)
        sign = pair_sign(8)

        def prepare(g, _):
            count = cycles[s, 0, g]
            cos, sin = turn((place_in * count) % LENGTH)
            ramp_cos[s, g] = cos
            ramp_sin[s, g] = sin * sign
            whole = jnp.full((8, LANES), (count * (4 * LANES)) % LENGTH, jnp.int32)
            cos, sin = turn(whole)
            step_cos[s, g] = cos
            step_sin[s, g] = sin * sign
            phase = jnp.full((8, LANES), phases[s, 0, g], jnp.float32)
            turn_cos[s, g] = jnp.cos(phase)
            turn_sin[s, g] = jnp.sin(phase) * sign
            return 0
        lax.fori_loop(lo, hi, prepare, 0)

    def prepare_slots():
        def one(o, _):
            low, high = jnp.int32(ROWS), jnp.int32(ROWS)
            for g in reversed(range(ROWS)):
                hit = targets[g] == o
                high = jnp.where(hit, low, high)
                low = jnp.where(hit, g, low)
            slot_row[CAP * o] = low
            slot_row[CAP * o + 1] = high
            return 0
        lax.fori_loop(0, BEAMS, one, 0)

        def clear(g, _):
            for s in range(2):
                proj[s, g, pl.ds(SUBL, PAD), :] = jnp.zeros((PAD, LANES), jnp.float32)
            return 0
        lax.fori_loop(0, ROWS, clear, 0)

    def forward(s, w, t):
        if t > 0:
            last = landing[s][w][t - 1]
            pltpu.make_async_copy(last, last, part_recv.at[s, w, t - 1]).wait()
        if t == STEPS:
            return
        for e in range(4):
            q = (e + 3) % 4
            if t < PARTS:
                held = pulse_hbm if t == 0 else block_ref
                own = held.at[s, pl.ds(4 * q + LP * w, LP), pl.ds(t * PS, PS), :]
            if t == 0:
                source = own
            else:
                value = last[table[place[s] + e]]
                if t < PARTS:
                    value = jnp.where(root[s], own[...], value)
                source = stage.at[s, w, t - 1, e]
                source[...] = value
            pltpu.make_async_remote_copy(
                src_ref=source, dst_ref=landing[s][w][t].at[e], send_sem=part_send, recv_sem=part_recv.at[s, w, t],
                device_id=peers[e], device_id_type=MESH).start()

    def assemble(s, c):
        for r in range(4):
            way = table[place[s] + 4 + r]
            late = table[place[s] + 8 + r]
            for p in range(4):
                own = block_ref[s, 4 * r + p, pl.ds(c * PS, PS), :]
                value = landing[s][p // LP][c][way, p % LP]
                for d in range(1, DEPTH):
                    value = jnp.where(late == d, landing[s][p // LP][c + d][way, p % LP], value)
                value = jnp.where(root[s], own, value)
                got[4 * r + p] = value
                got_turned[4 * r + p] = swapped(value) * pair_sign(PS)

    def project(s, c):
        def half(h, _):
            acc = [None] * 8
            for p in range(PB):
                b = got[p]
                t = got_turned[p]
                for k in range(8):
                    g = h * 8 + k
                    term = weights[s, 0, g, 0, p] * b + weights[s, 0, g, 1, p] * t
                    acc[k] = term if acc[k] is None else acc[k] + term
            for k in range(8):
                g = h * 8 + k
                off = offsets[s, 0, g] % LANES
                proj[s, g, pl.ds(c * PS, PS), :] = pltpu.roll(acc[k], (LANES - off) % LANES, 1)
            return 0
        lax.fori_loop(0, 2, half, 0)

    def added(s, g, k):
        lo, n = BOUNDS[k], BOUNDS[k + 1] - BOUNDS[k]
        wide = n + 8
        lane = lax.broadcasted_iota(jnp.int32, (wide, LANES), 1)
        off = offsets[s, 0, g]
        start = lo + 2 * (off // LANES)
        inside = lane < LANES - off % LANES
        u0 = proj[s, g, pl.ds(start, wide), :]
        u1 = proj[s, g, pl.ds(start + 2, wide), :]
        u2 = proj[s, g, pl.ds(start + 4, wide), :]
        here = jnp.where(inside, u0, u1)
        following = jnp.where(inside, u1, u2)
        moved = [here]
        for i in range(1, 4):
            moved.append(pltpu.roll(jnp.where(lane < i, following, here), LANES - i, 1))
        near = taps[s, 0, 0, g] * here[:n]
        far = taps[s, 0, 4, g] * here
        for i in range(1, 4):
            near = near + taps[s, 0, i, g] * moved[i][:n]
            far = far + taps[s, 0, 4 + i, g] * moved[i]
        shifted[g, pl.ds(0, wide), :] = far
        beyond = shifted[g, pl.ds(2, n), :]
        acc = near + pltpu.roll(jnp.where(lane[:n] < 4, beyond, far[:n]), LANES - 4, 1)
        ramped[g, pl.ds(8, n), :] = acc
        even = lax.broadcasted_iota(jnp.int32, (n, LANES), 0) % 2 == 0
        turned = jnp.where(even, ramped[g, pl.ds(9, n), :], ramped[g, pl.ds(7, n), :])
        cos, sin = ramp_cos[s, g], ramp_sin[s, g]
        cos_by, sin_by = step_cos[s, g], step_sin[s, g]
        parts = []
        for v in range(n // 8):
            parts.append(acc[v * 8 : v * 8 + 8] * cos + turned[v * 8 : v * 8 + 8] * sin)
            cos, sin = cos * cos_by - sin * sin_by, sin * cos_by + cos * sin_by
        ramp_cos[s, g] = cos
        ramp_sin[s, g] = sin
        return jnp.concatenate(parts, axis=0)

    def span(k):
        return pl.ds(BOUNDS[k], BOUNDS[k + 1] - BOUNDS[k])

    def copy_core(k):
        return pltpu.make_async_remote_copy(
            src_ref=first.at[:, span(k), :], dst_ref=first_in.at[:, span(k), :],
            send_sem=core_send.at[k], recv_sem=core_recv.at[k], device_id=core_peer, device_id_type=MESH)

    def copy_y(k):
        return pltpu.make_async_remote_copy(
            src_ref=second.at[:, span(k), :], dst_ref=second_in.at[:, span(k), :],
            send_sem=y_send.at[k], recv_sem=y_recv.at[k], device_id=y_peer, device_id_type=MESH)

    def copy_own(k):
        return pltpu.make_async_copy(
            slots.at[pl.ds(me * CAP, CAP), span(k), :], out_ref.at[pl.ds(me * CAP, CAP), span(k), :], own_sem.at[k])

    def rotated(value, s, g):
        n = value.shape[0] // 8
        y = value.reshape(n, 8, LANES)
        t = swapped(value).reshape(n, 8, LANES)
        return (y * turn_cos[s, g][None] + t * turn_sin[s, g][None]).reshape(value.shape)

    def begin(k):
        def row0(g, _):
            first[g, span(k), :] = sub_ref[g, span(k), :] + added(0, g, k)
            return 0
        lax.fori_loop(0, ROWS, row0, 0, unroll=8)
        copy_core(k).start()

    def extend(k):
        def row1(g, _):
            second[g, span(k), :] = first[g, span(k), :] + added(1, g, k)
            return 0
        lax.fori_loop(0, ROWS, row1, 0, unroll=8)

    def meet(k):
        copy_core(k).wait_recv()

        def row(g, _):
            second[g, span(k), :] = second[g, span(k), :] + rotated(first_in[g, span(k), :], 0, g)
            return 0
        lax.fori_loop(0, ROWS, row, 0, unroll=4)
        copy_y(k).start()

    def finish(k):
        copy_y(k).wait_recv()
        n = BOUNDS[k + 1] - BOUNDS[k]

        def row(g, _):
            merged[g, pl.ds(0, n), :] = second[g, span(k), :] + rotated(second_in[g, span(k), :], 1, g)
            return 0
        lax.fori_loop(0, ROWS, row, 0, unroll=4)

        def slot(q, _):
            g = slot_row[q]
            value = merged[jnp.minimum(g, ROWS - 1), pl.ds(0, n), :]
            slots[q, span(k), :] = jnp.where(g < ROWS, value, 0.0)
            return 0
        lax.fori_loop(0, SLOTS, slot, 0, unroll=8)

        def send(shift, _):
            to = me ^ shift
            pltpu.make_async_remote_copy(
                src_ref=slots.at[pl.ds(to * CAP, CAP), span(k), :],
                dst_ref=out_ref.at[pl.ds(me * CAP, CAP), span(k), :],
                send_sem=beam_send, recv_sem=beam_recv, device_id=(sub, to), device_id_type=MESH).start()
            return 0
        lax.fori_loop(1, BEAMS, send, 0)
        copy_own(k).start()

    pl.semaphore_wait(barrier, BEAMS + 1)
    def ready(s, k):
        assemble(s, k)
        project(s, k)

    def section0(k):
        if k < PARTS:
            ready(0, k)
        begin(k)

    def section1(k):
        if k < PARTS:
            ready(1, k)
        extend(k)

    for fetch in fetches:
        fetch.wait()
    place = []
    for s in range(2):
        o = owner[s]
        place.append((((x - o // 4) & 3) * 4 + ((z - o % 4) & 3)) * 12)
    root = [place[s] == 0 for s in range(2)]

    early = (STEPS - DEPTH) // 2
    pieces = [functools.partial(prepare_rows, s, h * 8, h * 8 + 8) for s in range(2) for h in range(2)]
    pieces += [prepare_slots] + [None] * (2 * DEPTH - 5)
    for k in range(early + 1):
        pieces += [functools.partial(ready, 0, k), functools.partial(begin, k)]
        pieces += [functools.partial(ready, 1, k), functools.partial(extend, k)]
    for t in range(STEPS + 1):
        if t == 1:
            for load in loads:
                load.wait()
        for s in range(2):
            for w in range(LINES):
                forward(s, w, t)
            k, odd = divmod(t - DEPTH, 2)
            if s == 0 and odd == 0 and 0 < k:
                meet(k - 1)
            if s == 0 and t == STEPS:
                finish(0)
            piece = pieces[2 * t + s]
            if piece is not None:
                piece()
    for piece in pieces[2 * STEPS + 2 :]:
        piece()
    finish(1)
    meet(early)
    for k in range(early + 1, CHUNKS):
        section0(k)
        finish(k - 2)
        section1(k)
        meet(k)
    finish(CHUNKS - 2)
    finish(CHUNKS - 1)

    for s in range(2):
        own = block_ref.at[s, :, pl.ds(0, PS), :]
        pltpu.make_async_copy(own, own, part_send).wait()
        pltpu.make_async_copy(stage.at[s], stage.at[s], part_send).wait()
    for k in range(CHUNKS):
        copy_core(k).wait_send()
        copy_y(k).wait_send()
        copy_own(k).wait()
    rest = slots.at[pl.ds(0, SLOTS - CAP)]
    pltpu.make_async_copy(rest, rest, beam_send).wait()
    landed = out_ref.at[pl.ds(0, SLOTS - CAP)]
    pltpu.make_async_copy(landed, landed, beam_recv).wait()


def call(*operands):
    hbm = pl.BlockSpec(memory_space=pl.ANY)

    def vmem(*shape):
        return pltpu.VMEM((*shape, LANES), jnp.float32)

    return pl.pallas_call(
        kernel,
        out_shape=jax.ShapeDtypeStruct((SLOTS, SUBL, LANES), jnp.float32),
        in_specs=[hbm] * (SMALL + 2),
        out_specs=hbm,
        scratch_shapes=[pltpu.SMEM(x.shape, x.dtype) for x in operands[:SMALL]] + [
            pltpu.SemaphoreType.DMA((SMALL,)),
        ] + [vmem(4, LP, PS)] * (2 * LINES * STEPS) + [
            vmem(2, LINES, STEPS - 1, 4, LP, PS),
            vmem(ROWS, SUBL),
            vmem(2, PB, SUBL),
            vmem(PB, PS),
            vmem(PB, PS),
            vmem(2, ROWS, SUBL + PAD),
            vmem(ROWS, PS + 8),
            vmem(ROWS, PS + 16),
            vmem(2, ROWS, 8),
            vmem(2, ROWS, 8),
            vmem(2, ROWS, 8),
            vmem(2, ROWS, 8),
            vmem(2, ROWS, 8),
            vmem(2, ROWS, 8),
            vmem(ROWS, SUBL),
            vmem(ROWS, SUBL),
            vmem(ROWS, SUBL),
            vmem(ROWS, SUBL),
            vmem(ROWS, PS),
            vmem(SLOTS, SUBL),
            pltpu.SMEM((SLOTS,), jnp.int32),
            pltpu.SemaphoreType.DMA((2,)),
            pltpu.SemaphoreType.DMA,
            pltpu.SemaphoreType.DMA((2, LINES, STEPS)),
            pltpu.SemaphoreType.DMA((CHUNKS,)),
            pltpu.SemaphoreType.DMA((CHUNKS,)),
            pltpu.SemaphoreType.DMA((CHUNKS,)),
            pltpu.SemaphoreType.DMA((CHUNKS,)),
            pltpu.SemaphoreType.DMA,
            pltpu.SemaphoreType.DMA,
            pltpu.SemaphoreType.DMA((CHUNKS,)),
        ],
        compiler_params=pltpu.CompilerParams(
            collective_id=1, has_side_effects=True, vmem_limit_bytes=56 * 2**20
        ),
    )(*operands)


def paired(x):
    lead = x.shape[:-2]
    n = len(lead)
    y = x.reshape(*lead, 2, SUBL // 2, LANES)
    y = y.transpose(*range(n), n + 1, n, n + 2)
    return y.reshape(*lead, SUBL, LANES)


def per_device(
    subimage, pulses, ingest_owner, weights, offsets, filter_taps, cycles, merge_phase, destination
):
    out = call(
        ingest_owner[:, 0], weights, offsets, filter_taps.transpose(0, 1, 3, 2), cycles, merge_phase, destination[:, 0], jnp.asarray(tree_table()),
        paired(subimage[0]), paired(pulses[:, 0, 0]),
    )
    out = out.reshape(SLOTS, SUBL // 2, 2, LANES).transpose(0, 2, 1, 3)
    return out.reshape(1, SLOTS, 2, LENGTH)


def solution(mesh):
    in_specs = (
        P("sub", "beam", None, None),
        P(None, "sub", "beam", None, None, None),
        P(None, "sub"),
        P(None, "sub", "beam", None, None),
        P(None, "sub", "beam"),
        P(None, "sub", "beam", None),
        P(None, "sub", "beam"),
        P(None, "sub", "beam"),
        P("beam", None),
    )
    out_specs = P("sub", "beam", None, None)
    return jax.shard_map(
        per_device, mesh=mesh, in_specs=in_specs, out_specs=out_specs, check_vma=False
    )
```
